512 devices in a mesh: row: 16 (over z), col: 32 (over x, y, core).
Axes of the slice: x: 4, y: 4, z: 16, core: 2. Of those that a mesh axis runs over, the one named last changes fastest.
Arguments:
- latent: bfloat16 [4, 192, 256, 256], P(None, 'row', 'col'), may hold values from -32 to 32
- group_gain: float32 [256], replicated, may hold values from 0.1 to 1.9
- group_shift: float32 [256], replicated, may hold values from -3 to 3
- kernel: bfloat16 [27, 256, 256], replicated, may hold values from -0.078125 to 0.078125
- kernel_bias: float32 [256], replicated, may hold values from -3 to 3
Outputs:
- features: bfloat16 [4, 192, 256, 256], P(None, 'row', 'col')
The draws below stay inside these ranges and needn't reach their ends.
All inputs are finite; a program needn't handle non-finite values.
Results may differ from the reference program's by a relative error of at most 0.0065.
Values may be sent and summed in bfloat16 or wider, within the bound.
A program may use at most 64 MiB of HBM per device.

```python
import jax
import jax.numpy as jnp
from jax import lax

CHANNELS = 256
GROUP_CH = 16
TAPS = 27
FRAMES = 4
HEIGHT = 192
WIDTH = 256


TWO_PI = 6.283185307179586


def draw_latent(key, part):
    key = jax.random.fold_in(key, 7)
    subkeys = jax.random.split(key, 9)
    vertical = jnp.arange(HEIGHT, dtype=jnp.float32) / max(HEIGHT - 1, 1)
    across = jnp.arange(WIDTH, dtype=jnp.float32) / max(WIDTH - 1, 1)
    flips = jax.random.uniform(subkeys[4], (2,), dtype=jnp.float32)
    vertical = jnp.where(flips[0] < 0.5, vertical, 1.0 - vertical)
    across = jnp.where(flips[1] < 0.5, across, 1.0 - across)
    mixing = jax.random.uniform(subkeys[5], (), dtype=jnp.float32, minval=0.2, maxval=0.8)
    trend = mixing * vertical[:, None] + (1.0 - mixing) * across[None, :]
    ramp_scale = jnp.exp(jnp.log(3.0) * 0.5 * (vertical[:, None] + across[None, :]))
    level = 1.5 * (1.0 + 2.0 * trend)
    waves = jax.random.uniform(subkeys[6], (4,), dtype=jnp.float32, minval=0.6, maxval=1.6)
    common_phase = jax.random.uniform(subkeys[7], (), dtype=jnp.float32, minval=0.0, maxval=TWO_PI)
    channel_phase = jax.random.uniform(subkeys[8], (CHANNELS,), dtype=jnp.float32, minval=0.0, maxval=TWO_PI)
    common_field = jnp.sin(TWO_PI * (waves[0] * vertical[:, None] + waves[1] * across[None, :]) + common_phase)
    channel_field = 0.6 * jnp.sin(TWO_PI * (waves[2] * vertical[:, None, None] - waves[3] * across[None, :, None]) + channel_phase)
    offset_field = common_field[:, :, None] + channel_field
    roughness = jnp.exp(jnp.log(10.0) * jax.random.uniform(subkeys[0], (FRAMES, HEIGHT, WIDTH, 1), dtype=jnp.float32))
    channel_scale = jnp.exp(jnp.log(10.0) * (jax.random.uniform(subkeys[1], (CHANNELS,), dtype=jnp.float32) - 0.5))
    centers = jax.random.uniform(subkeys[2], (CHANNELS,), dtype=jnp.float32, minval=-2.0, maxval=2.0)
    jitter = jax.random.truncated_normal(subkeys[3], -3.0, 3.0, (FRAMES, HEIGHT, WIDTH, CHANNELS), dtype=jnp.float32)
    smooth = level[:, :, None] + offset_field
    values = centers + smooth[None] + 0.07 * ramp_scale[None, :, :, None] * roughness * channel_scale * jitter
    return values.astype(jnp.bfloat16)


def normal_values(stream_key, extent, scale, bound, kind=jnp.bfloat16):
    return jnp.clip(scale * jax.random.normal(stream_key, extent, jnp.float32), -bound, bound).astype(kind)


def setup_inputs(seed: int = 0) -> dict:
    splits = jax.random.split(jax.random.key(seed), 6)
    return {
        "latent": draw_latent(jax.random.fold_in(splits[5], 71), 0),
        "group_gain": jnp.clip(1.0 + 0.18 * jax.random.normal(splits[1], (CHANNELS,), jnp.float32), 0.1, 1.9),
        "group_shift": normal_values(splits[2], (CHANNELS,), 0.5, 3.0, jnp.float32),
        "kernel": normal_values(splits[3], (TAPS, CHANNELS, CHANNELS), (TAPS * CHANNELS) ** -0.5, 0.078125),
        "kernel_bias": normal_values(splits[4], (CHANNELS,), 0.5, 3.0, jnp.float32),
    }


EPSILON = 1e-06

def normalize(inputs, group_gain, group_shift):
    frames, height, breadth, channels = inputs.shape
    groups = channels // GROUP_CH
    values = inputs.astype(jnp.float32).reshape(frames, height, breadth, groups, GROUP_CH)
    member_count = frames * height * breadth * GROUP_CH
    group_means = lax.optimization_barrier(jnp.sum(values, axis=(0, 1, 2, 4))) / member_count
    spread = values - group_means[:, None]
    variance = lax.optimization_barrier(jnp.sum(spread * spread, axis=(0, 1, 2, 4))) / member_count
    scaling = group_gain.reshape(groups, GROUP_CH) * lax.rsqrt(variance + EPSILON)[:, None]
    offsets = group_shift.reshape(groups, GROUP_CH) - group_means[:, None] * scaling
    normed = values * scaling + offsets
    return jax.nn.silu(normed).reshape(frames, height, breadth, channels).astype(jnp.bfloat16)

def reference(latent, group_gain, group_shift, kernel, kernel_bias):
    frames, height, breadth, channels = latent.shape
    active = normalize(latent, group_gain, group_shift)
    padded = jnp.pad(active, ((2, 0), (1, 1), (1, 1), (0, 0)), mode='edge')
    accumulated = jnp.zeros((frames * height * breadth, channels), jnp.float32)
    for time_tap in range(3):
        for row_tap in range(3):
            for col_tap in range(3):
                window = padded[time_tap:time_tap + frames, row_tap:row_tap + height, col_tap:col_tap + breadth]
                window = window.reshape(frames * height * breadth, channels)
                accumulated = accumulated + jnp.dot(window, kernel[9 * time_tap + 3 * row_tap + col_tap], preferred_element_type=jnp.float32)
    result = (accumulated + kernel_bias).astype(jnp.bfloat16)
    return result.reshape(frames, height, breadth, channels)
```

```python
import functools

import jax
import jax.numpy as jnp
from jax import lax
from jax.experimental import pallas as pl
from jax.experimental.pallas import tpu as pltpu
from jax.sharding import PartitionSpec as P

GROUP_CH = 16
EPSILON = 1e-06
MESH = pl.DeviceIdType.MESH
ROOT_ROW, ROOT_COL = 0, 1
F32 = jnp.float32


def group_total(values):
    lane = lax.broadcasted_iota(jnp.int32, values.shape, 1)
    for step in (1, 2, 4, 8):
        upper = (lane & step) != 0
        values = values + jnp.where(
            upper, pltpu.roll(values, step, 1), pltpu.roll(values, 128 - step, 1)
        )
    return values


def kernel(
    rows,
    cols,
    latent_hbm,
    gain_hbm,
    shift_hbm,
    weights_hbm,
    bias_hbm,
    out_ref,
    raw,
    gain_ref,
    shift_ref,
    bias_ref,
    weights,
    own,
    row_out,
    col_out,
    corner_out,
    row_in,
    col_in,
    corner_in,
    stat_row,
    gathered,
    params,
    windows,
    rims,
    patches,
    load_sem,
    halo_send,
    halo_recv,
    stat_send,
    stat_recv,
    param_send,
    param_recv,
):
    row, col = lax.axis_index("row"), lax.axis_index("col")
    devices = rows * cols
    me = row * cols + col
    is_root = jnp.logical_and(row == ROOT_ROW, col == ROOT_COL)
    up, down = lax.rem(row + rows - 1, rows), lax.rem(row + 1, rows)
    left, right = lax.rem(col + cols - 1, cols), lax.rem(col + 1, cols)

    load = pltpu.make_async_copy(latent_hbm, raw, load_sem.at[0])
    load.start()

    barrier = pltpu.get_barrier_semaphore()
    for r in (up, row, down):
        for c in (left, col, right):
            if r is not row or c is not col:
                pl.semaphore_signal(barrier, inc=1, device_id=(r, c), device_id_type=MESH)

    @pl.when(is_root)
    def _():
        def greet(i, carry):
            @pl.when(i != me)
            def _():
                pl.semaphore_signal(
                    barrier,
                    inc=1,
                    device_id=(lax.div(i, cols), lax.rem(i, cols)),
                    device_id_type=MESH,
                )

            return carry

        lax.fori_loop(0, devices, greet, 0)

    later = [
        pltpu.make_async_copy(source, target, load_sem.at[1 + i])
        for i, (source, target) in enumerate(
            (
                (gain_hbm, gain_ref),
                (shift_hbm, shift_ref),
                (bias_hbm, bias_ref),
                (weights_hbm, weights),
            )
        )
    ]
    for copy in later:
        copy.start()

    load.wait()
    values = raw[...].astype(F32)
    own[0] = values[:, :128]
    own[1] = values[:, 128:]
    count = values.shape[0]
    sums = jnp.sum(values, axis=0, keepdims=True)
    means = group_total(jnp.concatenate([sums[:, :128], sums[:, 128:]], axis=0)) * (
        1.0 / (count * GROUP_CH)
    )
    spread = values - jnp.concatenate([means[0:1], means[1:2]], axis=1)
    squares = jnp.sum(spread * spread, axis=0, keepdims=True)
    squares = group_total(jnp.concatenate([squares[:, :128], squares[:, 128:]], axis=0))
    part = lax.broadcasted_iota(jnp.int32, (1, 128), 1) & 12
    packed = jnp.where(
        part < 8,
        jnp.where(part == 0, means[0:1], means[1:2]),
        jnp.where(part == 8, squares[0:1], squares[1:2]),
    )
    stat_row[...] = packed.reshape(1, 1, 128)

    for t in range(4):
        row_out[0, t * 8 : t * 8 + 8] = values[t * 96 : t * 96 + 8]
        row_out[1, t * 8 : t * 8 + 8] = values[t * 96 + 88 : t * 96 + 96]
    for side, cell in ((0, 0), (1, 7)):
        for half in range(2):
            lanes = slice(half * 128, half * 128 + 128)
            col_out[side, :, lanes] = own[half, pl.ds(cell, 48, stride=8), :].astype(jnp.bfloat16)
            corner_out[side, 0:4, lanes] = own[half, pl.ds(cell, 4, stride=96), :]
            corner_out[2 + side, 0:4, lanes] = own[half, pl.ds(88 + cell, 4, stride=96), :]

    @pl.when(is_root)
    def _():
        pl.semaphore_wait(barrier, 8)
        gathered[pl.ds(me, 1)] = packed.reshape(1, 1, 128)

    @pl.when(jnp.logical_not(is_root))
    def _():
        pl.semaphore_wait(barrier, 9)
        pltpu.make_async_remote_copy(
            src_ref=stat_row,
            dst_ref=gathered.at[pl.ds(me, 1)],
            send_sem=stat_send,
            recv_sem=stat_recv,
            device_id=(ROOT_ROW, ROOT_COL),
            device_id_type=MESH,
        ).start()

    halos = []
    for source, target, device in (
        (row_out.at[0], row_in.at[1], (up, col)),
        (row_out.at[1], row_in.at[0], (down, col)),
        (col_out.at[0], col_in.at[1], (row, left)),
        (col_out.at[1], col_in.at[0], (row, right)),
        (corner_out.at[0], corner_in.at[3], (up, left)),
        (corner_out.at[1], corner_in.at[2], (up, right)),
        (corner_out.at[2], corner_in.at[1], (down, left)),
        (corner_out.at[3], corner_in.at[0], (down, right)),
    ):
        copy = pltpu.make_async_remote_copy(
            src_ref=source,
            dst_ref=target,
            send_sem=halo_send.at[len(halos)],
            recv_sem=halo_recv.at[len(halos)],
            device_id=device,
            device_id_type=MESH,
        )
        copy.start()
        halos.append(copy)

    for copy in halos:
        copy.wait_recv()

    at_row = (row == 0, row == rows - 1)
    at_col = (col == 0, col == cols - 1)
    for half in range(2):
        lanes = slice(half * 128, half * 128 + 128)
        for t in range(4):
            base = 8 + t * 112
            windows[1, half, base + 8 : base + 104] = own[half, t * 96 : t * 96 + 96]
            for side, at, edge in ((0, base, 0), (1, base + 104, 88)):
                windows[1, half, at : at + 8] = jnp.where(
                    at_row[side],
                    own[half, t * 96 + edge : t * 96 + edge + 8],
                    row_in[side, t * 8 : t * 8 + 8, lanes],
                )
        for side, cell in ((0, 0), (1, 7)):
            column = jnp.where(
                at_col[side],
                own[half, pl.ds(cell, 48, stride=8), :],
                col_in[side, :, lanes].astype(F32),
            )
            for t in range(4):
                rims[side, half, t * 14 + 1 : t * 14 + 13] = column[t * 12 : t * 12 + 12]
            for end, place, inner in ((0, 0, 1), (1, 13, 12)):
                rims[side, half, pl.ds(place, 4, stride=14), :] = jnp.where(
                    at_row[end],
                    rims[side, half, pl.ds(inner, 4, stride=14), :],
                    jnp.where(
                        at_col[side],
                        windows[1, half, pl.ds(8 + place * 8 + cell, 4, stride=112), :],
                        corner_in[2 * end + side, 0:4, lanes],
                    ),
                )
        for t in range(4):
            base = 8 + t * 112
            windows[0, half, base : base + 112] = windows[1, half, base - 1 : base + 111]
            windows[2, half, base : base + 112] = windows[1, half, base + 1 : base + 113]
        windows[0, half, pl.ds(8, 56, stride=8), :] = rims[0, half, 0:56]
        windows[2, half, pl.ds(15, 56, stride=8), :] = rims[1, half, 0:56]

    for copy in later:
        copy.wait()

    plane_root = col == ROOT_COL
    fan_out = params.at[0]

    def send_params(device):
        pltpu.make_async_remote_copy(
            src_ref=fan_out,
            dst_ref=fan_out,
            send_sem=param_send,
            recv_sem=param_recv,
            device_id=device,
            device_id_type=MESH,
        ).start()

    @pl.when(is_root)
    def _():
        incoming = gathered.at[pl.ds(0, devices - 1)]
        pltpu.make_async_copy(incoming, incoming, stat_recv).wait()
        stats = gathered[...].reshape(devices, 128)
        total = jnp.sum(stats, axis=0, keepdims=True)
        mean = total * (1.0 / devices)
        shift = stats - mean
        between = jnp.sum(shift * shift, axis=0, keepdims=True)
        lane = lax.broadcasted_iota(jnp.int32, (1, 128), 1)
        per_device = float(count * GROUP_CH)
        variance = (total + per_device * pltpu.roll(between, 8, 1)) * (
            1.0 / (devices * per_device)
        )
        merged = jnp.where((lane & 8) == 0, mean, variance)
        quarters = jnp.concatenate(
            [jnp.where((lane & 15) == 4 * q, merged, 0.0) for q in range(4)], axis=0
        )
        quarters = group_total(quarters)
        for half in range(2):
            scaling = gain_ref[half : half + 1] * lax.rsqrt(
                quarters[2 + half : 3 + half] + EPSILON
            )
            params[0, half : half + 1] = scaling
            params[0, 2 + half : 3 + half] = (
                shift_ref[half : half + 1] - quarters[half : half + 1] * scaling
            )

    @pl.when(jnp.logical_not(is_root))
    def _():
        pltpu.make_async_copy(fan_out, fan_out, param_recv).wait()

    @pl.when(plane_root)
    def _():
        def beside(i, carry):
            @pl.when(i != col)
            def _():
                send_params((row, i))

            return carry

        lax.fori_loop(0, cols, beside, 0)

    @pl.when(is_root)
    def _():
        def beyond(i, carry):
            @pl.when(i != row)
            def _():
                send_params((i, col))

            return carry

        lax.fori_loop(0, rows, beyond, 0)

    for c in range(3):
        for half in range(2):
            scaling = params[0, half : half + 1]
            offsets = params[0, 2 + half : 3 + half]
            for t in range(4):
                normed = windows[c, half, 8 + t * 112 : 120 + t * 112] * scaling + offsets
                halved = 0.5 * normed
                active = halved + halved * jnp.tanh(halved)
                even = active.astype(jnp.bfloat16)
                odd = active[8:104].astype(jnp.bfloat16)
                for b, cells in enumerate((even[0:96], odd, even[16:112])):
                    tap = (3 * b + c) * 256 + half * 128
                    patches[t * 96 : t * 96 + 96, tap : tap + 128] = cells

    bias = bias_ref[...]
    depth = 9 * 256
    newest = jnp.dot(patches[...], weights[2 * depth :], preferred_element_type=F32) + bias
    middle = jnp.dot(patches[0:288], weights[depth : 2 * depth], preferred_element_type=F32)
    oldest = jnp.dot(patches[0:192], weights[0:depth], preferred_element_type=F32)
    for t in range(4):
        m, o = max(t - 1, 0) * 96, max(t - 2, 0) * 96
        out_ref[t * 96 : t * 96 + 96] = (
            newest[t * 96 : t * 96 + 96] + middle[m : m + 96] + oldest[o : o + 96]
        ).astype(jnp.bfloat16)

    for copy in halos:
        copy.wait_send()

    @pl.when(jnp.logical_not(is_root))
    def _():
        pltpu.make_async_copy(stat_row, stat_row, stat_send).wait()

    @pl.when(plane_root)
    def _():
        sent = params.at[pl.ds(0, cols - 1)]
        pltpu.make_async_copy(sent, sent, param_send).wait()

    @pl.when(is_root)
    def _():
        sent = params.at[pl.ds(0, rows - 1)]
        pltpu.make_async_copy(sent, sent, param_send).wait()


def solution(mesh):
    rows, cols = mesh.shape["row"], mesh.shape["col"]

    def body(latent, group_gain, group_shift, taps, kernel_bias):
        frames, height, breadth, channels = latent.shape
        cells = frames * height * breadth
        vmem = pl.BlockSpec(memory_space=pltpu.VMEM)
        remote = pl.BlockSpec(memory_space=pltpu.HBM)
        result = pl.pallas_call(
            functools.partial(kernel, rows, cols),
            out_shape=jax.ShapeDtypeStruct((cells, channels), jnp.bfloat16),
            in_specs=[remote] * 5,
            out_specs=vmem,
            scratch_shapes=[
                pltpu.VMEM((cells, channels), jnp.bfloat16),
                pltpu.VMEM((2, 128), F32),
                pltpu.VMEM((2, 128), F32),
                pltpu.VMEM((1, channels), F32),
                pltpu.VMEM((27 * channels, channels), jnp.bfloat16),
                pltpu.VMEM((2, cells, 128), F32),
                pltpu.VMEM((2, 32, channels), F32),
                pltpu.VMEM((2, 48, channels), jnp.bfloat16),
                pltpu.VMEM((4, 8, channels), F32),
                pltpu.VMEM((2, 32, channels), F32),
                pltpu.VMEM((2, 48, channels), jnp.bfloat16),
                pltpu.VMEM((4, 8, channels), F32),
                pltpu.VMEM((1, 1, 128), F32),
                pltpu.VMEM((rows * cols, 1, 128), F32),
                pltpu.VMEM((cols, 8, 128), F32),
                pltpu.VMEM((3, 2, 464, 128), F32),
                pltpu.VMEM((2, 2, 64, 128), F32),
                pltpu.VMEM((cells, 9 * channels), jnp.bfloat16),
                pltpu.SemaphoreType.DMA((5,)),
                pltpu.SemaphoreType.DMA((8,)),
                pltpu.SemaphoreType.DMA((8,)),
                pltpu.SemaphoreType.DMA,
                pltpu.SemaphoreType.DMA,
                pltpu.SemaphoreType.DMA,
                pltpu.SemaphoreType.DMA,
            ],
            compiler_params=pltpu.CompilerParams(
                collective_id=0, has_side_effects=True, vmem_limit_bytes=64 * 2**20
            ),
        )(
            latent.reshape(cells, channels),
            group_gain.reshape(2, 128),
            group_shift.reshape(2, 128),
            taps.reshape(27 * channels, channels),
            kernel_bias.reshape(1, channels),
        )
        return result.reshape(frames, height, breadth, channels)

    return jax.shard_map(
        body,
        mesh=mesh,
        in_specs=(P(None, "row", "col", None), P(), P(), P(), P()),
        out_specs=P(None, "row", "col", None),
        check_vma=False,
    )
```

```python
import functools

import jax
import jax.numpy as jnp
from jax import lax
from jax.experimental import pallas as pl
from jax.experimental.pallas import tpu as pltpu
from jax.sharding import PartitionSpec as P

GROUP_CH = 16
EPSILON = 1e-06
MESH = pl.DeviceIdType.MESH
ROOT_ROW, ROOT_COL = 0, 1
NEAR = 3
F32 = jnp.float32


def fan_out_lists(rows, cols):
    def lateness(device):
        z, c = device
        return z + (c % 2 == 0) + 1.5 * (c // 8 == 3) + 1.5 * (c // 2 % 4 == 3)

    near = [(z, c) for z in range(NEAR) for c in range(cols)]
    near = [d for d in near if d != (ROOT_ROW, ROOT_COL)]
    near.sort(key=lateness)
    heads = [(z, ROOT_COL) for z in range(NEAR, rows)]
    return heads[:3] + near + heads[3:], [c for c in range(cols) if c != ROOT_COL]


def group_total(values):
    lane = lax.broadcasted_iota(jnp.int32, values.shape, 1) & 15
    for stride in (1, 4):
        total = values
        for step in (stride, 2 * stride, 3 * stride):
            total = total + jnp.where(
                lane >= step, pltpu.roll(values, step, 1), pltpu.roll(values, 112 + step, 1)
            )
        values = total
    return values


def halves(values):
    return jnp.concatenate([values[:, :128], values[:, 128:]], axis=0)


def kernel(
    rows,
    cols,
    latent_hbm,
    gain_hbm,
    shift_hbm,
    weights_hbm,
    bias_hbm,
    out_ref,
    raw,
    gain_ref,
    shift_ref,
    bias_ref,
    weights,
    own,
    row_out,
    col_out,
    corner_out,
    row_in,
    col_in,
    corner_in,
    stat_row,
    gathered,
    params,
    windows,
    rims,
    patches,
    load_sem,
    halo_send,
    halo_recv,
    stat_send,
    stat_recv,
    param_send,
    param_recv,
):
    row, col = lax.axis_index("row"), lax.axis_index("col")
    devices = rows * cols
    me = row * cols + col
    is_root = jnp.logical_and(row == ROOT_ROW, col == ROOT_COL)
    passes_on = jnp.logical_and(row >= NEAR, col == ROOT_COL)
    up, down = lax.rem(row + rows - 1, rows), lax.rem(row + 1, rows)
    left, right = lax.rem(col + cols - 1, cols), lax.rem(col + 1, cols)

    load = pltpu.make_async_copy(latent_hbm, raw, load_sem.at[0])
    load.start()

    barrier = pltpu.get_barrier_semaphore()
    for r in (up, row, down):
        for c in (left, col, right):
            if r is not row or c is not col:
                pl.semaphore_signal(barrier, inc=1, device_id=(r, c), device_id_type=MESH)

    @pl.when(is_root)
    def _():
        def greet(i, carry):
            far = lax.rem(rows // 2 + jnp.where(i & 1 == 0, i >> 1, rows - ((i + 1) >> 1)), rows)
            for c in range(cols):
                pl.semaphore_signal(barrier, inc=1, device_id=(far, c), device_id_type=MESH)
            return carry

        lax.fori_loop(0, rows - 1, greet, 0)
        for c in range(cols):
            if c != ROOT_COL:
                pl.semaphore_signal(
                    barrier, inc=1, device_id=(ROOT_ROW, c), device_id_type=MESH
                )

    later = [
        pltpu.make_async_copy(source, target, load_sem.at[1 + i])
        for i, (source, target) in enumerate(
            (
                (gain_hbm, gain_ref),
                (shift_hbm, shift_ref),
                (bias_hbm, bias_ref),
                (weights_hbm, weights),
            )
        )
    ]
    for copy in later:
        copy.start()

    load.wait()
    values = raw[...].astype(F32)
    own[0] = values[:, :128]
    own[1] = values[:, 128:]
    count = values.shape[0]
    cells = float(count * GROUP_CH)
    first = values[0:1]
    shifted = values - first
    sums = halves(jnp.sum(shifted, axis=0, keepdims=True))
    squares = halves(jnp.sum(shifted * shifted, axis=0, keepdims=True))
    squares = squares - sums * sums * (1.0 / count)
    first = halves(first)
    place = lax.broadcasted_iota(jnp.int32, (2, 128), 1) & 15
    base = jnp.where(place == 0, first, 0.0)
    for stride in (1, 4):
        base = base + sum(pltpu.roll(base, j * stride, 1) for j in (1, 2, 3))
    sums = sums + count * (first - base)
    squares = squares + sums * sums * (1.0 / count)
    totals = group_total(jnp.concatenate([sums, squares], axis=0))
    means = base + totals[0:2] * (1.0 / cells)
    squares = totals[2:4] - totals[0:2] * totals[0:2] * (1.0 / cells)
    part = lax.broadcasted_iota(jnp.int32, (1, 128), 1) & 12
    packed = jnp.where(
        part < 8,
        jnp.where(part == 0, means[0:1], means[1:2]),
        jnp.where(part == 8, squares[0:1], squares[1:2]),
    )
    stat_row[...] = packed

    for t in range(4):
        row_out[0, t * 8 : t * 8 + 8] = values[t * 96 : t * 96 + 8]
        row_out[1, t * 8 : t * 8 + 8] = values[t * 96 + 88 : t * 96 + 96]
    for side, cell in ((0, 0), (1, 7)):
        for half in range(2):
            lanes = slice(half * 128, half * 128 + 128)
            col_out[side, :, lanes] = own[half, pl.ds(cell, 48, stride=8), :].astype(jnp.bfloat16)
            corner_out[side, 0:4, lanes] = own[half, pl.ds(cell, 4, stride=96), :]
            corner_out[2 + side, 0:4, lanes] = own[half, pl.ds(88 + cell, 4, stride=96), :]

    @pl.when(is_root)
    def _():
        pl.semaphore_wait(barrier, 8)
        gathered[pl.ds(me, 1)] = packed

    @pl.when(jnp.logical_not(is_root))
    def _():
        pl.semaphore_wait(barrier, 9)
        pltpu.make_async_remote_copy(
            src_ref=stat_row,
            dst_ref=gathered.at[pl.ds(me, 1)],
            send_sem=stat_send,
            recv_sem=stat_recv,
            device_id=(ROOT_ROW, ROOT_COL),
            device_id_type=MESH,
        ).start()

    halos = []
    for source, target, device in (
        (row_out.at[0], row_in.at[1], (up, col)),
        (row_out.at[1], row_in.at[0], (down, col)),
        (col_out.at[0], col_in.at[1], (row, left)),
        (col_out.at[1], col_in.at[0], (row, right)),
        (corner_out.at[0], corner_in.at[3], (up, left)),
        (corner_out.at[1], corner_in.at[2], (up, right)),
        (corner_out.at[2], corner_in.at[1], (down, left)),
        (corner_out.at[3], corner_in.at[0], (down, right)),
    ):
        copy = pltpu.make_async_remote_copy(
            src_ref=source,
            dst_ref=target,
            send_sem=halo_send.at[len(halos)],
            recv_sem=halo_recv.at[len(halos)],
            device_id=device,
            device_id_type=MESH,
        )
        copy.start()
        halos.append(copy)

    for copy in halos:
        copy.wait_recv()

    at_row = (row == 0, row == rows - 1)
    at_col = (col == 0, col == cols - 1)
    for half in range(2):
        lanes = slice(half * 128, half * 128 + 128)
        for t in range(4):
            base = 8 + t * 112
            windows[1, half, base + 8 : base + 104] = own[half, t * 96 : t * 96 + 96]
            for side, at, edge in ((0, base, 0), (1, base + 104, 88)):
                windows[1, half, at : at + 8] = jnp.where(
                    at_row[side],
                    own[half, t * 96 + edge : t * 96 + edge + 8],
                    row_in[side, t * 8 : t * 8 + 8, lanes],
                )
        for side, cell in ((0, 0), (1, 7)):
            column = jnp.where(
                at_col[side],
                own[half, pl.ds(cell, 48, stride=8), :],
                col_in[side, :, lanes].astype(F32),
            )
            for t in range(4):
                rims[side, half, t * 14 + 1 : t * 14 + 13] = column[t * 12 : t * 12 + 12]
            for end, place, inner in ((0, 0, 1), (1, 13, 12)):
                rims[side, half, pl.ds(place, 4, stride=14), :] = jnp.where(
                    at_row[end],
                    rims[side, half, pl.ds(inner, 4, stride=14), :],
                    jnp.where(
                        at_col[side],
                        windows[1, half, pl.ds(8 + place * 8 + cell, 4, stride=112), :],
                        corner_in[2 * end + side, 0:4, lanes],
                    ),
                )
        for t in range(4):
            base = 8 + t * 112
            windows[0, half, base : base + 112] = windows[1, half, base - 1 : base + 111]
            windows[2, half, base : base + 112] = windows[1, half, base + 1 : base + 113]
        windows[0, half, pl.ds(8, 56, stride=8), :] = rims[0, half, 0:56]
        windows[2, half, pl.ds(15, 56, stride=8), :] = rims[1, half, 0:56]

    for copy in later:
        copy.wait()

    fan_out = params.at[0]

    def send_params(device):
        pltpu.make_async_remote_copy(
            src_ref=fan_out,
            dst_ref=fan_out,
            send_sem=param_send,
            recv_sem=param_recv,
            device_id=device,
            device_id_type=MESH,
        ).start()

    @pl.when(is_root)
    def _():
        incoming = gathered.at[pl.ds(0, devices - 1)]
        pltpu.make_async_copy(incoming, incoming, stat_recv).wait()
        lane = lax.broadcasted_iota(jnp.int32, (1, 128), 1) & 15
        base = jnp.where(lane < 8, packed, 0.0)
        shifted = gathered[...] - base
        sums = jnp.sum(shifted, axis=0, keepdims=True)
        between = jnp.sum(shifted * shifted, axis=0, keepdims=True)
        between = between - sums * sums * (1.0 / devices)
        variance = (sums + cells * pltpu.roll(between, 8, 1)) * (1.0 / (devices * cells))
        merged = jnp.where(
            lane < 8, base + sums * (1.0 / devices), lax.rsqrt(variance + EPSILON)
        )
        spread = []
        for q in range(4):
            quarter = jnp.where(lane >> 2 == q, merged, 0.0)
            spread.append(
                quarter + sum(pltpu.roll(quarter, 4 * (j - q) % 128, 1) for j in range(4) if j != q)
            )
        for half in range(2):
            scaling = gain_ref[half : half + 1] * spread[2 + half]
            params[0, half : half + 1] = scaling
            params[0, 2 + half : 3 + half] = shift_ref[half : half + 1] - spread[half] * scaling

    @pl.when(jnp.logical_not(is_root))
    def _():
        pltpu.make_async_copy(fan_out, fan_out, param_recv).wait()

    first_hand, in_plane = fan_out_lists(rows, cols)

    @pl.when(is_root)
    def _():
        for device in first_hand:
            send_params(device)

    @pl.when(passes_on)
    def _():
        for c in in_plane:
            send_params((row, c))

    for c in range(3):
        for half in range(2):
            scaling = params[0, half : half + 1]
            offsets = params[0, 2 + half : 3 + half]
            for t in range(4):
                normed = windows[c, half, 8 + t * 112 : 120 + t * 112] * scaling + offsets
                halved = 0.5 * normed
                active = halved + halved * jnp.tanh(halved)
                even = active.astype(jnp.bfloat16)
                odd = active[8:104].astype(jnp.bfloat16)
                for b, cells in enumerate((even[0:96], odd, even[16:112])):
                    tap = (3 * b + c) * 256 + half * 128
                    patches[t * 96 : t * 96 + 96, tap : tap + 128] = cells

    bias = bias_ref[...]
    depth = 9 * 256
    newest = jnp.dot(patches[...], weights[2 * depth :], preferred_element_type=F32) + bias
    middle = jnp.dot(patches[0:288], weights[depth : 2 * depth], preferred_element_type=F32)
    oldest = jnp.dot(patches[0:192], weights[0:depth], preferred_element_type=F32)
    for t in range(4):
        m, o = max(t - 1, 0) * 96, max(t - 2, 0) * 96
        out_ref[t * 96 : t * 96 + 96] = (
            newest[t * 96 : t * 96 + 96] + middle[m : m + 96] + oldest[o : o + 96]
        ).astype(jnp.bfloat16)

    for copy in halos:
        copy.wait_send()

    @pl.when(jnp.logical_not(is_root))
    def _():
        pltpu.make_async_copy(stat_row, stat_row, stat_send).wait()

    for sender, count in (
        (is_root, len(first_hand)),
        (passes_on, len(in_plane)),
    ):

        @pl.when(sender)
        def _(count=count):
            sent = params.at[pl.ds(0, count)]
            pltpu.make_async_copy(sent, sent, param_send).wait()


def solution(mesh):
    rows, cols = mesh.shape["row"], mesh.shape["col"]

    def body(latent, group_gain, group_shift, taps, kernel_bias):
        frames, height, breadth, channels = latent.shape
        cells = frames * height * breadth
        vmem = pl.BlockSpec(memory_space=pltpu.VMEM)
        remote = pl.BlockSpec(memory_space=pltpu.HBM)
        result = pl.pallas_call(
            functools.partial(kernel, rows, cols),
            out_shape=jax.ShapeDtypeStruct((cells, channels), jnp.bfloat16),
            in_specs=[remote] * 5,
            out_specs=vmem,
            scratch_shapes=[
                pltpu.VMEM((cells, channels), jnp.bfloat16),
                pltpu.VMEM((2, 128), F32),
                pltpu.VMEM((2, 128), F32),
                pltpu.VMEM((1, channels), F32),
                pltpu.VMEM((27 * channels, channels), jnp.bfloat16),
                pltpu.VMEM((2, cells, 128), F32),
                pltpu.VMEM((2, 32, channels), F32),
                pltpu.VMEM((2, 48, channels), jnp.bfloat16),
                pltpu.VMEM((4, 8, channels), F32),
                pltpu.VMEM((2, 32, channels), F32),
                pltpu.VMEM((2, 48, channels), jnp.bfloat16),
                pltpu.VMEM((4, 8, channels), F32),
                pltpu.VMEM((1, 128), F32),
                pltpu.VMEM((rows * cols, 128), F32),
                pltpu.VMEM((max(map(len, fan_out_lists(rows, cols))), 4, 128), F32),
                pltpu.VMEM((3, 2, 464, 128), F32),
                pltpu.VMEM((2, 2, 64, 128), F32),
                pltpu.VMEM((cells, 9 * channels), jnp.bfloat16),
                pltpu.SemaphoreType.DMA((5,)),
                pltpu.SemaphoreType.DMA((8,)),
                pltpu.SemaphoreType.DMA((8,)),
                pltpu.SemaphoreType.DMA,
                pltpu.SemaphoreType.DMA,
                pltpu.SemaphoreType.DMA,
                pltpu.SemaphoreType.DMA,
            ],
            compiler_params=pltpu.CompilerParams(
                collective_id=0, has_side_effects=True, vmem_limit_bytes=48 * 2**20
            ),
        )(
            pltpu.with_memory_space_constraint(latent.reshape(cells, channels), pltpu.HBM),
            pltpu.with_memory_space_constraint(group_gain.reshape(2, 128), pltpu.HBM),
            pltpu.with_memory_space_constraint(group_shift.reshape(2, 128), pltpu.HBM),
            pltpu.with_memory_space_constraint(taps.reshape(27 * channels, channels), pltpu.HBM),
            pltpu.with_memory_space_constraint(kernel_bias.reshape(1, channels), pltpu.HBM),
        )
        return result.reshape(frames, height, breadth, channels)

    return jax.shard_map(
        body,
        mesh=mesh,
        in_specs=(P(None, "row", "col", None), P(), P(), P(), P()),
        out_specs=P(None, "row", "col", None),
        check_vma=False,
    )
```

```python
import functools

import jax
import jax.numpy as jnp
from jax import lax
from jax.experimental import pallas as pl
from jax.experimental.pallas import tpu as pltpu
from jax.sharding import PartitionSpec as P

GROUP_CH = 16
EPSILON = 1e-06
MESH = pl.DeviceIdType.MESH
ROOT_ROW, ROOT_COL = 0, 1
NEAR = 3
SIDES = (64, 112)
CORNERS = (160, 168, 176, 184)
F32 = jnp.float32


def fan_out_lists(rows, cols):
    def lateness(device):
        z, c = device
        x, y = c // 8, c // 2 % 4
        return (0, 2, 3)[z] + (z == 0 and max(x, y) == 3) - 0.5 * (z > 0 and x == 3)

    near = [(z, c) for z in range(NEAR) for c in range(cols)]
    near = [d for d in near if d != (ROOT_ROW, ROOT_COL)]
    near.sort(key=lateness)
    heads = [(z, ROOT_COL) for z in range(NEAR, rows)]
    return heads[:4] + near[:64] + heads[4:] + near[64:], [c for c in range(cols) if c != ROOT_COL]


def group_total(values):
    lane = lax.broadcasted_iota(jnp.int32, values.shape, 1) & 15
    for stride in (1, 4):
        total = values
        for step in (stride, 2 * stride, 3 * stride):
            total = total + jnp.where(
                lane >= step, pltpu.roll(values, step, 1), pltpu.roll(values, 112 + step, 1)
            )
        values = total
    return values


def halves(values):
    return jnp.concatenate([values[:, :128], values[:, 128:]], axis=0)


def kernel(
    rows,
    cols,
    latent_hbm,
    gain_hbm,
    shift_hbm,
    weights_hbm,
    bias_hbm,
    out_ref,
    raw,
    affine,
    weights,
    own,
    rim_out,
    rim_in,
    stat_row,
    gathered,
    merged_row,
    windows,
    rims,
    patches,
    load_sem,
    rim_send,
    rim_recv,
    stat_send,
    stat_recv,
    param_send,
    param_recv,
):
    row, col = lax.axis_index("row"), lax.axis_index("col")
    devices = rows * cols
    me = row * cols + col
    is_root = jnp.logical_and(row == ROOT_ROW, col == ROOT_COL)
    passes_on = jnp.logical_and(row >= NEAR, col == ROOT_COL)
    up, down = lax.rem(row + rows - 1, rows), lax.rem(row + 1, rows)
    left, right = lax.rem(col + cols - 1, cols), lax.rem(col + 1, cols)

    load = pltpu.make_async_copy(latent_hbm, raw, load_sem.at[0])
    load.start()

    barrier = pltpu.get_barrier_semaphore()
    for r in (up, row, down):
        for c in (left, col, right):
            if r is not row or c is not col:
                pl.semaphore_signal(barrier, inc=1, device_id=(r, c), device_id_type=MESH)

    @pl.when(is_root)
    def _():
        def greet(i, carry):
            far = lax.rem(rows // 2 + jnp.where(i & 1 == 0, i >> 1, rows - ((i + 1) >> 1)), rows)
            for c in range(cols):
                pl.semaphore_signal(barrier, inc=1, device_id=(far, c), device_id_type=MESH)
            return carry

        lax.fori_loop(0, rows - 1, greet, 0)
        for c in range(cols):
            if c != ROOT_COL:
                pl.semaphore_signal(
                    barrier, inc=1, device_id=(ROOT_ROW, c), device_id_type=MESH
                )

    for i, source in enumerate((gain_hbm, shift_hbm, bias_hbm)):
        pltpu.make_async_copy(source, affine.at[i], load_sem.at[1]).start()
    load_weights = pltpu.make_async_copy(weights_hbm, weights, load_sem.at[2])
    load_weights.start()

    load.wait()
    values = raw[...].astype(F32)
    own[0] = values[:, :128]
    own[1] = values[:, 128:]
    count = values.shape[0]
    cells = float(count * GROUP_CH)
    first = values[0:1]
    shifted = values - first
    sums = halves(jnp.sum(shifted, axis=0, keepdims=True))
    squares = halves(jnp.sum(shifted * shifted, axis=0, keepdims=True))
    squares = squares - sums * sums * (1.0 / count)
    first = halves(first)
    place = lax.broadcasted_iota(jnp.int32, (2, 128), 1) & 15
    base = jnp.where(place == 0, first, 0.0)
    for stride in (1, 4):
        base = base + sum(pltpu.roll(base, j * stride, 1) for j in (1, 2, 3))
    sums = sums + count * (first - base)
    squares = squares + sums * sums * (1.0 / count)
    totals = group_total(jnp.concatenate([sums, squares], axis=0))
    means = base + totals[0:2] * (1.0 / cells)
    squares = totals[2:4] - totals[0:2] * totals[0:2] * (1.0 / cells)
    part = lax.broadcasted_iota(jnp.int32, (1, 128), 1) & 12
    packed = jnp.where(
        part < 8,
        jnp.where(part == 0, means[0:1], means[1:2]),
        jnp.where(part == 8, squares[0:1], squares[1:2]),
    )
    stat_row[...] = packed

    for t in range(4):
        rim_out[t * 8 : t * 8 + 8] = values[t * 96 : t * 96 + 8]
        rim_out[32 + t * 8 : 40 + t * 8] = values[t * 96 + 88 : t * 96 + 96]
    for side, cell in ((0, 0), (1, 7)):
        for half in range(2):
            lanes = slice(half * 128, half * 128 + 128)
            at = SIDES[side]
            rim_out[at : at + 48, lanes] = own[half, pl.ds(cell, 48, stride=8), :]
            for end, place in ((0, 0), (1, 88)):
                at = CORNERS[2 * end + side]
                rim_out[at : at + 4, lanes] = own[half, pl.ds(place + cell, 4, stride=96), :]

    @pl.when(is_root)
    def _():
        pl.semaphore_wait(barrier, 8)
        gathered[pl.ds(me, 1)] = packed

    @pl.when(jnp.logical_not(is_root))
    def _():
        pl.semaphore_wait(barrier, 9)
        pltpu.make_async_remote_copy(
            src_ref=stat_row,
            dst_ref=gathered.at[pl.ds(me, 1)],
            send_sem=stat_send,
            recv_sem=stat_recv,
            device_id=(ROOT_ROW, ROOT_COL),
            device_id_type=MESH,
        ).start()

    for source, target, size, device in (
        (0, 32, 32, (up, col)),
        (32, 0, 32, (down, col)),
        (SIDES[0], SIDES[1], 48, (row, left)),
        (SIDES[1], SIDES[0], 48, (row, right)),
        (CORNERS[0], CORNERS[3], 8, (up, left)),
        (CORNERS[1], CORNERS[2], 8, (up, right)),
        (CORNERS[2], CORNERS[1], 8, (down, left)),
        (CORNERS[3], CORNERS[0], 8, (down, right)),
    ):
        pltpu.make_async_remote_copy(
            src_ref=rim_out.at[pl.ds(source, size)],
            dst_ref=rim_in.at[pl.ds(target, size)],
            send_sem=rim_send,
            recv_sem=rim_recv,
            device_id=device,
            device_id_type=MESH,
        ).start()

    pltpu.make_async_copy(rim_in, rim_in, rim_recv).wait()

    at_row = (row == 0, row == rows - 1)
    at_col = (col == 0, col == cols - 1)
    for half in range(2):
        lanes = slice(half * 128, half * 128 + 128)
        for t in range(4):
            base = 8 + t * 112
            windows[1, half, base + 8 : base + 104] = own[half, t * 96 : t * 96 + 96]
            for side, at, edge in ((0, base, 0), (1, base + 104, 88)):
                windows[1, half, at : at + 8] = jnp.where(
                    at_row[side],
                    own[half, t * 96 + edge : t * 96 + edge + 8],
                    rim_in[side * 32 + t * 8 : side * 32 + t * 8 + 8, lanes],
                )
        for side, cell in ((0, 0), (1, 7)):
            column = jnp.where(
                at_col[side],
                own[half, pl.ds(cell, 48, stride=8), :],
                rim_in[SIDES[side] : SIDES[side] + 48, lanes],
            )
            for t in range(4):
                rims[side, half, t * 14 + 1 : t * 14 + 13] = column[t * 12 : t * 12 + 12]
            for end, place, inner in ((0, 0, 1), (1, 13, 12)):
                corner = CORNERS[2 * end + side]
                rims[side, half, pl.ds(place, 4, stride=14), :] = jnp.where(
                    at_row[end],
                    rims[side, half, pl.ds(inner, 4, stride=14), :],
                    jnp.where(
                        at_col[side],
                        windows[1, half, pl.ds(8 + place * 8 + cell, 4, stride=112), :],
                        rim_in[corner : corner + 4, lanes],
                    ),
                )
        for t in range(4):
            base = 8 + t * 112
            windows[0, half, base : base + 112] = windows[1, half, base - 1 : base + 111]
            windows[2, half, base : base + 112] = windows[1, half, base + 1 : base + 113]
        windows[0, half, pl.ds(8, 56, stride=8), :] = rims[0, half, 0:56]
        windows[2, half, pl.ds(15, 56, stride=8), :] = rims[1, half, 0:56]

    pltpu.make_async_copy(affine, affine, load_sem.at[1]).wait()
    load_weights.wait()

    def send_params(device):
        pltpu.make_async_remote_copy(
            src_ref=merged_row,
            dst_ref=merged_row,
            send_sem=param_send,
            recv_sem=param_recv,
            device_id=device,
            device_id_type=MESH,
        ).start()

    @pl.when(is_root)
    def _():
        incoming = gathered.at[pl.ds(0, devices - 1)]
        pltpu.make_async_copy(incoming, incoming, stat_recv).wait()
        lane = lax.broadcasted_iota(jnp.int32, (1, 128), 1) & 15
        base = jnp.where(lane < 8, packed, 0.0)
        shifted = gathered[...] - base
        sums = jnp.sum(shifted, axis=0, keepdims=True)
        between = jnp.sum(shifted * shifted, axis=0, keepdims=True)
        between = between - sums * sums * (1.0 / devices)
        variance = (sums + cells * pltpu.roll(between, 8, 1)) * (1.0 / (devices * cells))
        merged = jnp.where(
            lane < 8, base + sums * (1.0 / devices), lax.rsqrt(variance + EPSILON)
        )
        merged_row[...] = merged

    @pl.when(jnp.logical_not(is_root))
    def _():
        pltpu.make_async_copy(merged_row, merged_row, param_recv).wait()

    first_hand, in_plane = fan_out_lists(rows, cols)

    @pl.when(is_root)
    def _():
        for device in first_hand:
            send_params(device)

    @pl.when(passes_on)
    def _():
        for c in in_plane:
            send_params((row, c))

    merged = merged_row[...]
    quarter = lax.broadcasted_iota(jnp.int32, (1, 128), 1) >> 2 & 3
    spread = []
    for q in range(4):
        part = jnp.where(quarter == q, merged, 0.0)
        spread.append(part + sum(pltpu.roll(part, 4 * (j - q) % 128, 1) for j in range(4) if j != q))
    scalings = [affine[0, half : half + 1] * spread[2 + half] for half in range(2)]
    offsets = [affine[1, half : half + 1] - spread[half] * scalings[half] for half in range(2)]

    depth = 9 * 256
    newest = middle = oldest = 0.0
    for c in range(3):
        for half in range(2):
            for t in range(4):
                normed = windows[c, half, 8 + t * 112 : 120 + t * 112] * scalings[half] + offsets[half]
                halved = 0.5 * normed
                active = halved + halved * jnp.tanh(halved)
                even = active.astype(jnp.bfloat16)
                odd = active[8:104].astype(jnp.bfloat16)
                for b, cells in enumerate((even[0:96], odd, even[16:112])):
                    tap = (3 * b + c) * 256 + half * 128
                    patches[t * 96 : t * 96 + 96, tap : tap + 128] = cells
        for b in range(3):
            tap = (3 * b + c) * 256
            taps = slice(tap, tap + 256)
            newest += jnp.dot(
                patches[:, taps],
                weights[2 * depth + tap : 2 * depth + tap + 256],
                preferred_element_type=F32,
            )
            middle += jnp.dot(
                patches[0:288, taps],
                weights[depth + tap : depth + tap + 256],
                preferred_element_type=F32,
            )
            oldest += jnp.dot(
                patches[0:192, taps], weights[tap : tap + 256], preferred_element_type=F32
            )
    newest += jnp.concatenate([affine[2, 0:1], affine[2, 1:2]], axis=1)
    for t in range(4):
        m, o = max(t - 1, 0) * 96, max(t - 2, 0) * 96
        out_ref[t * 96 : t * 96 + 96] = (
            newest[t * 96 : t * 96 + 96] + middle[m : m + 96] + oldest[o : o + 96]
        ).astype(jnp.bfloat16)

    pltpu.make_async_copy(rim_out, rim_out, rim_send).wait()

    @pl.when(jnp.logical_not(is_root))
    def _():
        pltpu.make_async_copy(stat_row, stat_row, stat_send).wait()

    for sender, count in (
        (is_root, len(first_hand)),
        (passes_on, len(in_plane)),
    ):

        @pl.when(sender)
        def _(count=count):
            sent = gathered.at[pl.ds(0, count)]
            pltpu.make_async_copy(sent, sent, param_send).wait()


def solution(mesh):
    rows, cols = mesh.shape["row"], mesh.shape["col"]

    def body(latent, group_gain, group_shift, taps, kernel_bias):
        frames, height, breadth, channels = latent.shape
        cells = frames * height * breadth
        vmem = pl.BlockSpec(memory_space=pltpu.VMEM)
        remote = pl.BlockSpec(memory_space=pltpu.HBM)
        result = pl.pallas_call(
            functools.partial(kernel, rows, cols),
            out_shape=jax.ShapeDtypeStruct((cells, channels), jnp.bfloat16),
            in_specs=[remote] * 5,
            out_specs=vmem,
            scratch_shapes=[
                pltpu.VMEM((cells, channels), jnp.bfloat16),
                pltpu.VMEM((3, 2, 128), F32),
                pltpu.VMEM((27 * channels, channels), jnp.bfloat16),
                pltpu.VMEM((2, cells, 128), F32),
                pltpu.VMEM((192, channels), F32),
                pltpu.VMEM((192, channels), F32),
                pltpu.VMEM((1, 128), F32),
                pltpu.VMEM((rows * cols, 128), F32),
                pltpu.VMEM((1, 128), F32),
                pltpu.VMEM((3, 2, 464, 128), F32),
                pltpu.VMEM((2, 2, 64, 128), F32),
                pltpu.VMEM((cells, 9 * channels), jnp.bfloat16),
                pltpu.SemaphoreType.DMA((3,)),
                pltpu.SemaphoreType.DMA,
                pltpu.SemaphoreType.DMA,
                pltpu.SemaphoreType.DMA,
                pltpu.SemaphoreType.DMA,
                pltpu.SemaphoreType.DMA,
                pltpu.SemaphoreType.DMA,
            ],
            compiler_params=pltpu.CompilerParams(
                collective_id=0, has_side_effects=True, vmem_limit_bytes=48 * 2**20
            ),
        )(
            pltpu.with_memory_space_constraint(latent.reshape(cells, channels), pltpu.HBM),
            pltpu.with_memory_space_constraint(group_gain.reshape(2, 128), pltpu.HBM),
            pltpu.with_memory_space_constraint(group_shift.reshape(2, 128), pltpu.HBM),
            pltpu.with_memory_space_constraint(taps.reshape(27 * channels, channels), pltpu.HBM),
            pltpu.with_memory_space_constraint(kernel_bias.reshape(2, 128), pltpu.HBM),
        )
        return result.reshape(frames, height, breadth, channels)

    return jax.shard_map(
        body,
        mesh=mesh,
        in_specs=(P(None, "row", "col", None), P(), P(), P(), P()),
        out_specs=P(None, "row", "col", None),
        check_vma=False,
    )
```

```python
import functools

import jax
import jax.numpy as jnp
from jax import lax
from jax.experimental import pallas as pl
from jax.experimental.pallas import tpu as pltpu
from jax.sharding import PartitionSpec as P

GROUP_CH = 16
EPSILON = 1e-06
MESH = pl.DeviceIdType.MESH
SIDES = (64, 112)
CORNERS = (160, 168, 176, 184)
F32 = jnp.float32


SERVED = {
    1: (0,),
    9: (4, 8, 5, 9),
    3: (1, 2, 6, 10),
    25: (12, 13, 14, 15),
    7: (3, 7, 11),
}


def roots_of(cols):
    if cols == 32:
        return SERVED
    return {1: (), 0: tuple(range(cols // 2))}


def group_total(values):
    lane = lax.broadcasted_iota(jnp.int32, values.shape, 1) & 15
    for stride in (1, 4):
        total = values
        for step in (stride, 2 * stride, 3 * stride):
            total = total + jnp.where(
                lane >= step, pltpu.roll(values, step, 1), pltpu.roll(values, 112 + step, 1)
            )
        values = total
    return values


def halves(values):
    return jnp.concatenate([values[:, :128], values[:, 128:]], axis=0)


def kernel(
    rows,
    cols,
    latent_hbm,
    gain_hbm,
    shift_hbm,
    weights_hbm,
    bias_hbm,
    out_ref,
    raw,
    affine,
    weights,
    own,
    rim_out,
    rim_in,
    stat_row,
    gathered,
    merged_row,
    windows,
    rims,
    patches,
    load_sem,
    rim_send,
    rim_recv,
    stat_send,
    stat_recv,
    param_send,
    param_recv,
):
    row, col = lax.axis_index("row"), lax.axis_index("col")
    devices = rows * cols
    me = row * cols + col
    served = roots_of(cols)
    is_root = functools.reduce(jnp.logical_or, [me == r for r in served])
    up, down = lax.rem(row + rows - 1, rows), lax.rem(row + 1, rows)
    left, right = lax.rem(col + cols - 1, cols), lax.rem(col + 1, cols)

    load = pltpu.make_async_copy(latent_hbm, raw, load_sem.at[0])
    load.start()

    barrier = pltpu.get_barrier_semaphore()
    for r in (up, row, down):
        for c in (left, col, right):
            if r is not row or c is not col:
                pl.semaphore_signal(barrier, inc=1, device_id=(r, c), device_id_type=MESH)

    @pl.when(is_root)
    def _():
        def greet(i, carry):
            far = lax.rem(rows // 2 + jnp.where(i & 1 == 0, i >> 1, rows - ((i + 1) >> 1)), rows)
            for c in range(cols):
                pl.semaphore_signal(barrier, inc=1, device_id=(far, c), device_id_type=MESH)
            return carry

        lax.fori_loop(0, rows - 1, greet, 0)
        for offset in range(1, cols):
            pl.semaphore_signal(
                barrier, inc=1, device_id=(0, (col + offset) & (cols - 1)), device_id_type=MESH
            )

    for i, source in enumerate((gain_hbm, shift_hbm, bias_hbm)):
        pltpu.make_async_copy(source, affine.at[i], load_sem.at[1]).start()
    load_weights = pltpu.make_async_copy(weights_hbm, weights, load_sem.at[2])
    load_weights.start()

    load.wait()
    values = raw[...].astype(F32)
    own[0] = values[:, :128]
    own[1] = values[:, 128:]
    count = values.shape[0]
    cells = float(count * GROUP_CH)
    first = values[0:1]
    shifted = values - first
    sums = halves(jnp.sum(shifted, axis=0, keepdims=True))
    squares = halves(jnp.sum(shifted * shifted, axis=0, keepdims=True))
    squares = squares - sums * sums * (1.0 / count)
    first = halves(first)
    place = lax.broadcasted_iota(jnp.int32, (2, 128), 1) & 15
    base = jnp.where(place == 0, first, 0.0)
    for stride in (1, 4):
        base = base + sum(pltpu.roll(base, j * stride, 1) for j in (1, 2, 3))
    sums = sums + count * (first - base)
    squares = squares + sums * sums * (1.0 / count)
    totals = group_total(jnp.concatenate([sums, squares], axis=0))
    means = base + totals[0:2] * (1.0 / cells)
    squares = totals[2:4] - totals[0:2] * totals[0:2] * (1.0 / cells)
    part = lax.broadcasted_iota(jnp.int32, (1, 128), 1) & 12
    packed = jnp.where(
        part < 8,
        jnp.where(part == 0, means[0:1], means[1:2]),
        jnp.where(part == 8, squares[0:1], squares[1:2]),
    )
    stat_row[...] = packed

    for t in range(4):
        rim_out[t * 8 : t * 8 + 8] = values[t * 96 : t * 96 + 8]
        rim_out[32 + t * 8 : 40 + t * 8] = values[t * 96 + 88 : t * 96 + 96]
    for side, cell in ((0, 0), (1, 7)):
        for half in range(2):
            lanes = slice(half * 128, half * 128 + 128)
            at = SIDES[side]
            rim_out[at : at + 48, lanes] = own[half, pl.ds(cell, 48, stride=8), :]
            for end, place in ((0, 0), (1, 88)):
                at = CORNERS[2 * end + side]
                rim_out[at : at + 4, lanes] = own[half, pl.ds(place + cell, 4, stride=96), :]

    def send_stats(c):
        pltpu.make_async_remote_copy(
            src_ref=stat_row,
            dst_ref=gathered.at[pl.ds(me, 1)],
            send_sem=stat_send,
            recv_sem=stat_recv,
            device_id=(0, c),
            device_id_type=MESH,
        ).start()

    @pl.when(is_root)
    def _():
        pl.semaphore_wait(barrier, 7 + len(served))
        gathered[pl.ds(me, 1)] = packed
        for r in served:
            pl.when(me != r)(functools.partial(send_stats, r))

    @pl.when(jnp.logical_not(is_root))
    def _():
        pl.semaphore_wait(barrier, 8 + len(served))
        for r in served:
            send_stats(r)

    for source, target, size, device in (
        (0, 32, 32, (up, col)),
        (32, 0, 32, (down, col)),
        (SIDES[0], SIDES[1], 48, (row, left)),
        (SIDES[1], SIDES[0], 48, (row, right)),
        (CORNERS[0], CORNERS[3], 8, (up, left)),
        (CORNERS[1], CORNERS[2], 8, (up, right)),
        (CORNERS[2], CORNERS[1], 8, (down, left)),
        (CORNERS[3], CORNERS[0], 8, (down, right)),
    ):
        pltpu.make_async_remote_copy(
            src_ref=rim_out.at[pl.ds(source, size)],
            dst_ref=rim_in.at[pl.ds(target, size)],
            send_sem=rim_send,
            recv_sem=rim_recv,
            device_id=device,
            device_id_type=MESH,
        ).start()

    pltpu.make_async_copy(rim_in, rim_in, rim_recv).wait()

    at_row = (row == 0, row == rows - 1)
    at_col = (col == 0, col == cols - 1)
    for half in range(2):
        lanes = slice(half * 128, half * 128 + 128)
        for t in range(4):
            base = 8 + t * 112
            windows[1, half, base + 8 : base + 104] = own[half, t * 96 : t * 96 + 96]
            for side, at, edge in ((0, base, 0), (1, base + 104, 88)):
                windows[1, half, at : at + 8] = jnp.where(
                    at_row[side],
                    own[half, t * 96 + edge : t * 96 + edge + 8],
                    rim_in[side * 32 + t * 8 : side * 32 + t * 8 + 8, lanes],
                )
        for side, cell in ((0, 0), (1, 7)):
            column = jnp.where(
                at_col[side],
                own[half, pl.ds(cell, 48, stride=8), :],
                rim_in[SIDES[side] : SIDES[side] + 48, lanes],
            )
            for t in range(4):
                rims[side, half, t * 14 + 1 : t * 14 + 13] = column[t * 12 : t * 12 + 12]
            for end, place, inner in ((0, 0, 1), (1, 13, 12)):
                corner = CORNERS[2 * end + side]
                rims[side, half, pl.ds(place, 4, stride=14), :] = jnp.where(
                    at_row[end],
                    rims[side, half, pl.ds(inner, 4, stride=14), :],
                    jnp.where(
                        at_col[side],
                        windows[1, half, pl.ds(8 + place * 8 + cell, 4, stride=112), :],
                        rim_in[corner : corner + 4, lanes],
                    ),
                )
        for t in range(4):
            base = 8 + t * 112
            windows[0, half, base : base + 112] = windows[1, half, base - 1 : base + 111]
            windows[2, half, base : base + 112] = windows[1, half, base + 1 : base + 113]
        windows[0, half, pl.ds(8, 56, stride=8), :] = rims[0, half, 0:56]
        windows[2, half, pl.ds(15, 56, stride=8), :] = rims[1, half, 0:56]

    pltpu.make_async_copy(affine, affine, load_sem.at[1]).wait()
    load_weights.wait()

    def send_params(device):
        pltpu.make_async_remote_copy(
            src_ref=merged_row,
            dst_ref=merged_row,
            send_sem=param_send,
            recv_sem=param_recv,
            device_id=device,
            device_id_type=MESH,
        ).start()

    @pl.when(is_root)
    def _():
        incoming = gathered.at[pl.ds(0, devices - 1)]
        pltpu.make_async_copy(incoming, incoming, stat_recv).wait()
        lane = lax.broadcasted_iota(jnp.int32, (1, 128), 1) & 15
        base = jnp.where(lane < 8, packed, 0.0)
        shifted = gathered[...] - base
        sums = jnp.sum(shifted, axis=0, keepdims=True)
        between = jnp.sum(shifted * shifted, axis=0, keepdims=True)
        between = between - sums * sums * (1.0 / devices)
        variance = (sums + cells * pltpu.roll(between, 8, 1)) * (1.0 / (devices * cells))
        merged = jnp.where(
            lane < 8, base + sums * (1.0 / devices), lax.rsqrt(variance + EPSILON)
        )
        merged_row[...] = merged

    @pl.when(jnp.logical_not(is_root))
    def _():
        pltpu.make_async_copy(merged_row, merged_row, param_recv).wait()

    def targets(r):
        return [
            (z, 2 * chip + core)
            for z in range(rows)
            for chip in served[r]
            for core in (1, 0)
            if z > 0 or 2 * chip + core not in served
        ]

    for r in served:

        @pl.when(me == r)
        def _(r=r):
            for device in targets(r):
                send_params(device)

    merged = merged_row[...]
    quarter = lax.broadcasted_iota(jnp.int32, (1, 128), 1) >> 2 & 3
    spread = []
    for q in range(4):
        part = jnp.where(quarter == q, merged, 0.0)
        spread.append(part + sum(pltpu.roll(part, 4 * (j - q) % 128, 1) for j in range(4) if j != q))
    scalings = [affine[0, half : half + 1] * spread[2 + half] for half in range(2)]
    offsets = [affine[1, half : half + 1] - spread[half] * scalings[half] for half in range(2)]

    depth = 9 * 256
    newest = middle = oldest = 0.0
    for c in range(3):
        for half in range(2):
            for t in range(4):
                normed = windows[c, half, 8 + t * 112 : 120 + t * 112] * scalings[half] + offsets[half]
                halved = 0.5 * normed
                active = halved + halved * jnp.tanh(halved)
                even = active.astype(jnp.bfloat16)
                odd = active[8:104].astype(jnp.bfloat16)
                for b, cells in enumerate((even[0:96], odd, even[16:112])):
                    tap = (3 * b + c) * 256 + half * 128
                    patches[t * 96 : t * 96 + 96, tap : tap + 128] = cells
        for b in range(3):
            tap = (3 * b + c) * 256
            taps = slice(tap, tap + 256)
            newest += jnp.dot(
                patches[:, taps],
                weights[2 * depth + tap : 2 * depth + tap + 256],
                preferred_element_type=F32,
            )
            middle += jnp.dot(
                patches[0:288, taps],
                weights[depth + tap : depth + tap + 256],
                preferred_element_type=F32,
            )
            oldest += jnp.dot(
                patches[0:192, taps], weights[tap : tap + 256], preferred_element_type=F32
            )
    newest += jnp.concatenate([affine[2, 0:1], affine[2, 1:2]], axis=1)
    for t in range(4):
        m, o = max(t - 1, 0) * 96, max(t - 2, 0) * 96
        out_ref[t * 96 : t * 96 + 96] = (
            newest[t * 96 : t * 96 + 96] + middle[m : m + 96] + oldest[o : o + 96]
        ).astype(jnp.bfloat16)

    pltpu.make_async_copy(rim_out, rim_out, rim_send).wait()

    def wait_rows(count, semaphore):
        sent = gathered.at[pl.ds(0, count)]
        pltpu.make_async_copy(sent, sent, semaphore).wait()

    @pl.when(is_root)
    def _():
        wait_rows(len(served) - 1, stat_send)

    @pl.when(jnp.logical_not(is_root))
    def _():
        wait_rows(len(served), stat_send)

    for r in served:
        if targets(r):

            @pl.when(me == r)
            def _(r=r):
                wait_rows(len(targets(r)), param_send)


def solution(mesh):
    rows, cols = mesh.shape["row"], mesh.shape["col"]

    def body(latent, group_gain, group_shift, taps, kernel_bias):
        frames, height, breadth, channels = latent.shape
        cells = frames * height * breadth
        vmem = pl.BlockSpec(memory_space=pltpu.VMEM)
        remote = pl.BlockSpec(memory_space=pltpu.HBM)
        result = pl.pallas_call(
            functools.partial(kernel, rows, cols),
            out_shape=jax.ShapeDtypeStruct((cells, channels), jnp.bfloat16),
            in_specs=[remote] * 5,
            out_specs=vmem,
            scratch_shapes=[
                pltpu.VMEM((cells, channels), jnp.bfloat16),
                pltpu.VMEM((3, 2, 128), F32),
                pltpu.VMEM((27 * channels, channels), jnp.bfloat16),
                pltpu.VMEM((2, cells, 128), F32),
                pltpu.VMEM((192, channels), F32),
                pltpu.VMEM((192, channels), F32),
                pltpu.VMEM((1, 128), F32),
                pltpu.VMEM((rows * cols, 128), F32),
                pltpu.VMEM((1, 128), F32),
                pltpu.VMEM((3, 2, 464, 128), F32),
                pltpu.VMEM((2, 2, 64, 128), F32),
                pltpu.VMEM((cells, 9 * channels), jnp.bfloat16),
                pltpu.SemaphoreType.DMA((3,)),
                pltpu.SemaphoreType.DMA,
                pltpu.SemaphoreType.DMA,
                pltpu.SemaphoreType.DMA,
                pltpu.SemaphoreType.DMA,
                pltpu.SemaphoreType.DMA,
                pltpu.SemaphoreType.DMA,
            ],
            compiler_params=pltpu.CompilerParams(
                collective_id=0, has_side_effects=True, vmem_limit_bytes=48 * 2**20
            ),
        )(
            pltpu.with_memory_space_constraint(latent.reshape(cells, channels), pltpu.HBM),
            pltpu.with_memory_space_constraint(group_gain.reshape(2, 128), pltpu.HBM),
            pltpu.with_memory_space_constraint(group_shift.reshape(2, 128), pltpu.HBM),
            pltpu.with_memory_space_constraint(taps.reshape(27 * channels, channels), pltpu.HBM),
            pltpu.with_memory_space_constraint(kernel_bias.reshape(2, 128), pltpu.HBM),
        )
        return result.reshape(frames, height, breadth, channels)

    return jax.shard_map(
        body,
        mesh=mesh,
        in_specs=(P(None, "row", "col", None), P(), P(), P(), P()),
        out_specs=P(None, "row", "col", None),
        check_vma=False,
    )
```

```python
import functools

import jax
import jax.numpy as jnp
from jax import lax
from jax.experimental import pallas as pl
from jax.experimental.pallas import tpu as pltpu
from jax.sharding import PartitionSpec as P

GROUP_CH = 16
EPSILON = 1e-06
MESH = pl.DeviceIdType.MESH
SIDES = (64, 112)
CORNERS = (160, 168, 176, 184)
F32 = jnp.float32


SERVED = {
    1: (0,),
    9: (4, 8, 5, 9),
    3: (1, 2, 6, 10),
    25: (12, 13, 14, 15),
    7: (3, 7, 11),
}


def roots_of(cols):
    if cols == 32:
        return SERVED
    return {1: (), 0: tuple(range(cols // 2))}


def group_total(values):
    lane = lax.broadcasted_iota(jnp.int32, values.shape, 1) & 15
    for stride in (1, 4):
        total = values
        for step in (stride, 2 * stride, 3 * stride):
            total = total + jnp.where(
                lane >= step, pltpu.roll(values, step, 1), pltpu.roll(values, 112 + step, 1)
            )
        values = total
    return values


def halves(values):
    return jnp.concatenate([values[:, :128], values[:, 128:]], axis=0)


def kernel(
    rows,
    cols,
    latent_hbm,
    gain_hbm,
    shift_hbm,
    weights_hbm,
    bias_hbm,
    out_ref,
    raw,
    affine,
    weights,
    own,
    rim_out,
    rim_in,
    stat_row,
    gathered,
    merged_row,
    windows,
    rims,
    patches,
    load_sem,
    rim_send,
    rim_recv,
    stat_send,
    stat_recv,
    param_send,
    param_recv,
):
    row, col = lax.axis_index("row"), lax.axis_index("col")
    devices = rows * cols
    me = row * cols + col
    served = roots_of(cols)
    is_root = functools.reduce(jnp.logical_or, [me == r for r in served])
    up, down = lax.rem(row + rows - 1, rows), lax.rem(row + 1, rows)
    left, right = lax.rem(col + cols - 1, cols), lax.rem(col + 1, cols)

    loads = [
        pltpu.make_async_copy(
            latent_hbm.at[pl.ds(part * 192, 192)], raw.at[pl.ds(part * 192, 192)], load_sem.at[part]
        )
        for part in range(2)
    ]
    for load in loads:
        load.start()

    barrier = pltpu.get_barrier_semaphore()
    for r in (up, row, down):
        for c in (left, col, right):
            if r is not row or c is not col:
                pl.semaphore_signal(barrier, inc=1, device_id=(r, c), device_id_type=MESH)

    @pl.when(is_root)
    def _():
        def greet(i, carry):
            far = lax.rem(rows // 2 + jnp.where(i & 1 == 0, i >> 1, rows - ((i + 1) >> 1)), rows)
            for c in range(cols):
                pl.semaphore_signal(barrier, inc=1, device_id=(far, c), device_id_type=MESH)
            return carry

        lax.fori_loop(0, rows - 1, greet, 0)
        for offset in range(1, cols):
            pl.semaphore_signal(
                barrier, inc=1, device_id=(0, (col + offset) & (cols - 1)), device_id_type=MESH
            )

    for i, source in enumerate((gain_hbm, shift_hbm, bias_hbm)):
        pltpu.make_async_copy(source, affine.at[i], load_sem.at[2]).start()
    load_weights = pltpu.make_async_copy(weights_hbm, weights, load_sem.at[3])
    load_weights.start()

    count = raw.shape[0]
    cells = float(count * GROUP_CH)
    loads[0].wait()
    first = raw[0:16].astype(F32)[0:1]
    sums = squares = 0.0
    for part in range(2):
        if part:
            loads[part].wait()
        shifted = raw[part * 192 : part * 192 + 192].astype(F32) - first
        shifted = shifted.reshape(24, 8, shifted.shape[1])
        sums = sums + jnp.sum(shifted, axis=0)
        squares = squares + jnp.sum(shifted * shifted, axis=0)
    sums = halves(jnp.sum(sums, axis=0, keepdims=True))
    squares = halves(jnp.sum(squares, axis=0, keepdims=True))
    squares = squares - sums * sums * (1.0 / count)
    first = halves(first)
    place = lax.broadcasted_iota(jnp.int32, (2, 128), 1) & 15
    base = jnp.where(place == 0, first, 0.0)
    for stride in (1, 4):
        base = base + sum(pltpu.roll(base, j * stride, 1) for j in (1, 2, 3))
    sums = sums + count * (first - base)
    squares = squares + sums * sums * (1.0 / count)
    totals = group_total(jnp.concatenate([sums, squares], axis=0))
    means = base + totals[0:2] * (1.0 / cells)
    squares = totals[2:4] - totals[0:2] * totals[0:2] * (1.0 / cells)
    part = lax.broadcasted_iota(jnp.int32, (1, 128), 1) & 12
    packed = jnp.where(
        part < 8,
        jnp.where(part == 0, means[0:1], means[1:2]),
        jnp.where(part == 8, squares[0:1], squares[1:2]),
    )
    stat_row[...] = packed

    def send_stats(c):
        pltpu.make_async_remote_copy(
            src_ref=stat_row,
            dst_ref=gathered.at[pl.ds(me, 1)],
            send_sem=stat_send,
            recv_sem=stat_recv,
            device_id=(0, c),
            device_id_type=MESH,
        ).start()

    @pl.when(is_root)
    def _():
        pl.semaphore_wait(barrier, 7 + len(served))
        gathered[pl.ds(me, 1)] = packed
        for r in served:
            pl.when(me != r)(functools.partial(send_stats, r))

    @pl.when(jnp.logical_not(is_root))
    def _():
        pl.semaphore_wait(barrier, 8 + len(served))
        for r in served:
            send_stats(r)

    values = raw[...].astype(F32)
    own[0, 0:count] = values[:, :128]
    own[1, 0:count] = values[:, 128:]
    for t in range(4):
        rim_out[t * 8 : t * 8 + 8] = values[t * 96 : t * 96 + 8]
        rim_out[32 + t * 8 : 40 + t * 8] = values[t * 96 + 88 : t * 96 + 96]
    for side, cell in ((0, 0), (1, 7)):
        for half in range(2):
            lanes = slice(half * 128, half * 128 + 128)
            at = SIDES[side]
            rim_out[at : at + 48, lanes] = own[half, pl.ds(cell, 48, stride=8), :]
            for end, place in ((0, 0), (1, 88)):
                at = CORNERS[2 * end + side]
                rim_out[at : at + 4, lanes] = own[half, pl.ds(place + cell, 4, stride=96), :]

    for source, target, size, device in (
        (0, 32, 32, (up, col)),
        (32, 0, 32, (down, col)),
        (SIDES[0], SIDES[1], 48, (row, left)),
        (SIDES[1], SIDES[0], 48, (row, right)),
        (CORNERS[0], CORNERS[3], 8, (up, left)),
        (CORNERS[1], CORNERS[2], 8, (up, right)),
        (CORNERS[2], CORNERS[1], 8, (down, left)),
        (CORNERS[3], CORNERS[0], 8, (down, right)),
    ):
        pltpu.make_async_remote_copy(
            src_ref=rim_out.at[pl.ds(source, size)],
            dst_ref=rim_in.at[pl.ds(target, size)],
            send_sem=rim_send,
            recv_sem=rim_recv,
            device_id=device,
            device_id_type=MESH,
        ).start()

    pltpu.make_async_copy(rim_in, rim_in, rim_recv).wait()

    at_row = (row == 0, row == rows - 1)
    at_col = (col == 0, col == cols - 1)
    for half in range(2):
        lanes = slice(half * 128, half * 128 + 128)
        for t in range(4):
            base = 8 + t * 112
            windows[1, half, base + 8 : base + 104] = own[half, t * 96 : t * 96 + 96]
            for side, at, edge in ((0, base, 0), (1, base + 104, 88)):
                windows[1, half, at : at + 8] = jnp.where(
                    at_row[side],
                    own[half, t * 96 + edge : t * 96 + edge + 8],
                    rim_in[side * 32 + t * 8 : side * 32 + t * 8 + 8, lanes],
                )
        for side, cell in ((0, 0), (1, 7)):
            column = jnp.where(
                at_col[side],
                own[half, pl.ds(cell, 48, stride=8), :],
                rim_in[SIDES[side] : SIDES[side] + 48, lanes],
            )
            for t in range(4):
                rims[side, half, t * 14 + 1 : t * 14 + 13] = column[t * 12 : t * 12 + 12]
            for end, place, inner in ((0, 0, 1), (1, 13, 12)):
                corner = CORNERS[2 * end + side]
                rims[side, half, pl.ds(place, 4, stride=14), :] = jnp.where(
                    at_row[end],
                    rims[side, half, pl.ds(inner, 4, stride=14), :],
                    jnp.where(
                        at_col[side],
                        windows[1, half, pl.ds(8 + place * 8 + cell, 4, stride=112), :],
                        rim_in[corner : corner + 4, lanes],
                    ),
                )
        for t in range(4):
            base = 8 + t * 112
            windows[0, half, base : base + 112] = windows[1, half, base - 1 : base + 111]
            windows[2, half, base : base + 112] = windows[1, half, base + 1 : base + 113]
        windows[0, half, pl.ds(8, 56, stride=8), :] = rims[0, half, 0:56]
        windows[2, half, pl.ds(15, 56, stride=8), :] = rims[1, half, 0:56]

    pltpu.make_async_copy(affine, affine, load_sem.at[2]).wait()
    load_weights.wait()

    def send_params(device):
        pltpu.make_async_remote_copy(
            src_ref=merged_row,
            dst_ref=merged_row,
            send_sem=param_send,
            recv_sem=param_recv,
            device_id=device,
            device_id_type=MESH,
        ).start()

    @pl.when(is_root)
    def _():
        incoming = gathered.at[pl.ds(0, devices - 1)]
        pltpu.make_async_copy(incoming, incoming, stat_recv).wait()
        lane = lax.broadcasted_iota(jnp.int32, (1, 128), 1) & 15
        base = jnp.where(lane < 8, packed, 0.0)
        shifted = gathered[0:devices] - base
        sums = jnp.sum(shifted, axis=0, keepdims=True)
        between = jnp.sum(shifted * shifted, axis=0, keepdims=True)
        between = between - sums * sums * (1.0 / devices)
        variance = (sums + cells * pltpu.roll(between, 8, 1)) * (1.0 / (devices * cells))
        merged = jnp.where(
            lane < 8, base + sums * (1.0 / devices), lax.rsqrt(variance + EPSILON)
        )
        merged_row[...] = merged

    @pl.when(jnp.logical_not(is_root))
    def _():
        pltpu.make_async_copy(merged_row, merged_row, param_recv).wait()

    def targets(r):
        return [
            (z, 2 * chip + core)
            for z in range(rows)
            for chip in served[r]
            for core in (1, 0)
            if z > 0 or 2 * chip + core not in served
        ]

    for r in served:

        @pl.when(me == r)
        def _(r=r):
            for device in targets(r):
                send_params(device)

    merged = merged_row[...]
    quarter = lax.broadcasted_iota(jnp.int32, (1, 128), 1) >> 2 & 3
    spread = []
    for q in range(4):
        part = jnp.where(quarter == q, merged, 0.0)
        spread.append(part + sum(pltpu.roll(part, 4 * (j - q) % 128, 1) for j in range(4) if j != q))
    scalings = [affine[0, half : half + 1] * spread[2 + half] for half in range(2)]
    offsets = [affine[1, half : half + 1] - spread[half] * scalings[half] for half in range(2)]

    depth = 9 * 256
    newest = middle = oldest = 0.0
    for c in range(3):
        for half in range(2):
            for t in range(4):
                normed = windows[c, half, 8 + t * 112 : 120 + t * 112] * scalings[half] + offsets[half]
                halved = 0.5 * normed
                active = halved + halved * jnp.tanh(halved)
                even = active.astype(jnp.bfloat16)
                odd = active[8:104].astype(jnp.bfloat16)
                for b, cells in enumerate((even[0:96], odd, even[16:112])):
                    tap = (3 * b + c) * 256 + half * 128
                    patches[t * 96 : t * 96 + 96, tap : tap + 128] = cells
        for b in range(3):
            tap = (3 * b + c) * 256
            taps = slice(tap, tap + 256)
            newest += jnp.dot(
                patches[:, taps],
                weights[2 * depth + tap : 2 * depth + tap + 256],
                preferred_element_type=F32,
            )
            middle += jnp.dot(
                patches[0:288, taps],
                weights[depth + tap : depth + tap + 256],
                preferred_element_type=F32,
            )
            oldest += jnp.dot(
                patches[0:192, taps], weights[tap : tap + 256], preferred_element_type=F32
            )
    newest += jnp.concatenate([affine[2, 0:1], affine[2, 1:2]], axis=1)
    for t in range(4):
        m, o = max(t - 1, 0) * 96, max(t - 2, 0) * 96
        out_ref[t * 96 : t * 96 + 96] = (
            newest[t * 96 : t * 96 + 96] + middle[m : m + 96] + oldest[o : o + 96]
        ).astype(jnp.bfloat16)

    pltpu.make_async_copy(rim_out, rim_out, rim_send).wait()

    def wait_rows(count, semaphore):
        sent = gathered.at[pl.ds(0, count)]
        pltpu.make_async_copy(sent, sent, semaphore).wait()

    @pl.when(is_root)
    def _():
        wait_rows(len(served) - 1, stat_send)

    @pl.when(jnp.logical_not(is_root))
    def _():
        wait_rows(len(served), stat_send)

    for r in served:
        if targets(r):

            @pl.when(me == r)
            def _(r=r):
                wait_rows(len(targets(r)), param_send)


def solution(mesh):
    rows, cols = mesh.shape["row"], mesh.shape["col"]

    def body(latent, group_gain, group_shift, taps, kernel_bias):
        frames, height, breadth, channels = latent.shape
        cells = frames * height * breadth
        vmem = pl.BlockSpec(memory_space=pltpu.VMEM)
        remote = pl.BlockSpec(memory_space=pltpu.HBM)
        result = pl.pallas_call(
            functools.partial(kernel, rows, cols),
            out_shape=jax.ShapeDtypeStruct((cells, channels), jnp.bfloat16),
            in_specs=[remote] * 5,
            out_specs=vmem,
            scratch_shapes=[
                pltpu.VMEM((cells, channels), jnp.bfloat16),
                pltpu.VMEM((3, 2, 128), F32),
                pltpu.VMEM((27 * channels, channels), jnp.bfloat16),
                pltpu.VMEM((2, 768, 128), F32),
                pltpu.VMEM((192, channels), F32),
                pltpu.VMEM((192, channels), F32),
                pltpu.VMEM((1, 128), F32),
                pltpu.VMEM((rows * cols + 8, 128), F32),
                pltpu.VMEM((1, 128), F32),
                pltpu.VMEM((3, 2, 904, 128), F32),
                pltpu.VMEM((2, 2, 112, 128), F32),
                pltpu.VMEM((cells, 9 * channels), jnp.bfloat16),
                pltpu.SemaphoreType.DMA((4,)),
                pltpu.SemaphoreType.DMA,
                pltpu.SemaphoreType.DMA,
                pltpu.SemaphoreType.DMA,
                pltpu.SemaphoreType.DMA,
                pltpu.SemaphoreType.DMA,
                pltpu.SemaphoreType.DMA,
            ],
            compiler_params=pltpu.CompilerParams(
                collective_id=0, has_side_effects=True, vmem_limit_bytes=48 * 2**20
            ),
        )(
            pltpu.with_memory_space_constraint(latent.reshape(cells, channels), pltpu.HBM),
            pltpu.with_memory_space_constraint(group_gain.reshape(2, 128), pltpu.HBM),
            pltpu.with_memory_space_constraint(group_shift.reshape(2, 128), pltpu.HBM),
            pltpu.with_memory_space_constraint(taps.reshape(27 * channels, channels), pltpu.HBM),
            pltpu.with_memory_space_constraint(kernel_bias.reshape(2, 128), pltpu.HBM),
        )
        return result.reshape(frames, height, breadth, channels)

    return jax.shard_map(
        body,
        mesh=mesh,
        in_specs=(P(None, "row", "col", None), P(), P(), P(), P()),
        out_specs=P(None, "row", "col", None),
        check_vma=False,
    )
```

```python
import functools

import jax
import jax.numpy as jnp
from jax import lax
from jax.experimental import pallas as pl
from jax.experimental.pallas import tpu as pltpu
from jax.sharding import PartitionSpec as P

GROUP_CH = 16
EPSILON = 1e-06
MESH = pl.DeviceIdType.MESH
SIDES = (64, 112)
CORNERS = (160, 168, 176, 184)
F32 = jnp.float32


SERVED = {
    1: (0,),
    9: (4, 8, 5, 9),
    3: (1, 2, 6, 10),
    25: (12, 13, 14, 15),
    7: (3, 7, 11),
}


def roots_of(cols):
    if cols == 32:
        return SERVED
    return {1: (), 0: tuple(range(cols // 2))}


def group_total(values):
    lane = lax.broadcasted_iota(jnp.int32, values.shape, 1) & 15
    for stride in (1, 4):
        total = values
        for step in (stride, 2 * stride, 3 * stride):
            total = total + jnp.where(
                lane >= step, pltpu.roll(values, step, 1), pltpu.roll(values, 112 + step, 1)
            )
        values = total
    return values


def halves(values):
    return jnp.concatenate([values[:, :128], values[:, 128:]], axis=0)


def kernel(
    rows,
    cols,
    latent_hbm,
    gain_hbm,
    shift_hbm,
    weights_hbm,
    bias_hbm,
    out_ref,
    raw,
    affine,
    weights,
    own,
    rim_out,
    rim_in,
    stat_row,
    gathered,
    merged_row,
    windows,
    rims,
    patches,
    load_sem,
    rim_send,
    rim_recv,
    stat_send,
    stat_recv,
    param_send,
    param_recv,
):
    row, col = lax.axis_index("row"), lax.axis_index("col")
    devices = rows * cols
    me = row * cols + col
    served = roots_of(cols)
    is_root = functools.reduce(jnp.logical_or, [me == r for r in served])
    up, down = lax.rem(row + rows - 1, rows), lax.rem(row + 1, rows)
    left, right = lax.rem(col + cols - 1, cols), lax.rem(col + 1, cols)

    load = pltpu.make_async_copy(latent_hbm, raw, load_sem.at[0])
    load.start()

    barrier = pltpu.get_barrier_semaphore()
    for r in (up, row, down):
        for c in (left, col, right):
            if r is not row or c is not col:
                pl.semaphore_signal(barrier, inc=1, device_id=(r, c), device_id_type=MESH)

    @pl.when(is_root)
    def _():
        def greet(i, carry):
            far = lax.rem(rows // 2 + jnp.where(i & 1 == 0, i >> 1, rows - ((i + 1) >> 1)), rows)
            for c in range(cols):
                pl.semaphore_signal(barrier, inc=1, device_id=(far, c), device_id_type=MESH)
            return carry

        lax.fori_loop(0, rows - 1, greet, 0)
        for offset in range(1, cols):
            pl.semaphore_signal(
                barrier, inc=1, device_id=(0, (col + offset) & (cols - 1)), device_id_type=MESH
            )

    for i, source in enumerate((gain_hbm, shift_hbm, bias_hbm)):
        pltpu.make_async_copy(source, affine.at[i], load_sem.at[1]).start()
    load_weights = pltpu.make_async_copy(weights_hbm, weights, load_sem.at[2])
    load_weights.start()

    load.wait()
    values = raw[...].astype(F32)
    count = values.shape[0]
    own[0, 0:count] = values[:, :128]
    own[1, 0:count] = values[:, 128:]
    cells = float(count * GROUP_CH)
    first = values[0:1]
    shifted = values - first
    sums = halves(jnp.sum(shifted, axis=0, keepdims=True))
    squares = halves(jnp.sum(shifted * shifted, axis=0, keepdims=True))
    squares = squares - sums * sums * (1.0 / count)
    first = halves(first)
    place = lax.broadcasted_iota(jnp.int32, (2, 128), 1) & 15
    base = jnp.where(place == 0, first, 0.0)
    for stride in (1, 4):
        base = base + sum(pltpu.roll(base, j * stride, 1) for j in (1, 2, 3))
    sums = sums + count * (first - base)
    squares = squares + sums * sums * (1.0 / count)
    totals = group_total(jnp.concatenate([sums, squares], axis=0))
    means = base + totals[0:2] * (1.0 / cells)
    squares = totals[2:4] - totals[0:2] * totals[0:2] * (1.0 / cells)
    part = lax.broadcasted_iota(jnp.int32, (1, 128), 1) & 12
    packed = jnp.where(
        part < 8,
        jnp.where(part == 0, means[0:1], means[1:2]),
        jnp.where(part == 8, squares[0:1], squares[1:2]),
    )
    stat_row[...] = packed

    for t in range(4):
        rim_out[t * 8 : t * 8 + 8] = values[t * 96 : t * 96 + 8]
        rim_out[32 + t * 8 : 40 + t * 8] = values[t * 96 + 88 : t * 96 + 96]
    for side, cell in ((0, 0), (1, 7)):
        for half in range(2):
            lanes = slice(half * 128, half * 128 + 128)
            at = SIDES[side]
            rim_out[at : at + 48, lanes] = own[half, pl.ds(cell, 48, stride=8), :]
            for end, place in ((0, 0), (1, 88)):
                at = CORNERS[2 * end + side]
                rim_out[at : at + 4, lanes] = own[half, pl.ds(place + cell, 4, stride=96), :]

    def send_stats(c):
        pltpu.make_async_remote_copy(
            src_ref=stat_row,
            dst_ref=gathered.at[pl.ds(me, 1)],
            send_sem=stat_send,
            recv_sem=stat_recv,
            device_id=(0, c),
            device_id_type=MESH,
        ).start()

    @pl.when(is_root)
    def _():
        pl.semaphore_wait(barrier, 7 + len(served))
        gathered[pl.ds(me, 1)] = packed
        for r in served:
            pl.when(me != r)(functools.partial(send_stats, r))

    @pl.when(jnp.logical_not(is_root))
    def _():
        pl.semaphore_wait(barrier, 8 + len(served))
        for r in served:
            send_stats(r)

    for source, target, size, device in (
        (0, 32, 32, (up, col)),
        (32, 0, 32, (down, col)),
        (SIDES[0], SIDES[1], 48, (row, left)),
        (SIDES[1], SIDES[0], 48, (row, right)),
        (CORNERS[0], CORNERS[3], 8, (up, left)),
        (CORNERS[1], CORNERS[2], 8, (up, right)),
        (CORNERS[2], CORNERS[1], 8, (down, left)),
        (CORNERS[3], CORNERS[0], 8, (down, right)),
    ):
        pltpu.make_async_remote_copy(
            src_ref=rim_out.at[pl.ds(source, size)],
            dst_ref=rim_in.at[pl.ds(target, size)],
            send_sem=rim_send,
            recv_sem=rim_recv,
            device_id=device,
            device_id_type=MESH,
        ).start()

    pltpu.make_async_copy(rim_in, rim_in, rim_recv).wait()

    at_row = (row == 0, row == rows - 1)
    at_col = (col == 0, col == cols - 1)
    for half in range(2):
        lanes = slice(half * 128, half * 128 + 128)
        for t in range(4):
            base = 8 + t * 112
            windows[1, half, base + 8 : base + 104] = own[half, t * 96 : t * 96 + 96]
            for side, at, edge in ((0, base, 0), (1, base + 104, 88)):
                windows[1, half, at : at + 8] = jnp.where(
                    at_row[side],
                    own[half, t * 96 + edge : t * 96 + edge + 8],
                    rim_in[side * 32 + t * 8 : side * 32 + t * 8 + 8, lanes],
                )
        for side, cell in ((0, 0), (1, 7)):
            column = jnp.where(
                at_col[side],
                own[half, pl.ds(cell, 48, stride=8), :],
                rim_in[SIDES[side] : SIDES[side] + 48, lanes],
            )
            for t in range(4):
                rims[side, half, t * 14 + 1 : t * 14 + 13] = column[t * 12 : t * 12 + 12]
            for end, place, inner in ((0, 0, 1), (1, 13, 12)):
                corner = CORNERS[2 * end + side]
                rims[side, half, pl.ds(place, 4, stride=14), :] = jnp.where(
                    at_row[end],
                    rims[side, half, pl.ds(inner, 4, stride=14), :],
                    jnp.where(
                        at_col[side],
                        windows[1, half, pl.ds(8 + place * 8 + cell, 4, stride=112), :],
                        rim_in[corner : corner + 4, lanes],
                    ),
                )
        for t in range(4):
            base = 8 + t * 112
            windows[0, half, base : base + 112] = windows[1, half, base - 1 : base + 111]
            windows[2, half, base : base + 112] = windows[1, half, base + 1 : base + 113]
        windows[0, half, pl.ds(8, 56, stride=8), :] = rims[0, half, 0:56]
        windows[2, half, pl.ds(15, 56, stride=8), :] = rims[1, half, 0:56]

    pltpu.make_async_copy(affine, affine, load_sem.at[1]).wait()
    load_weights.wait()

    def send_params(device):
        pltpu.make_async_remote_copy(
            src_ref=merged_row,
            dst_ref=merged_row,
            send_sem=param_send,
            recv_sem=param_recv,
            device_id=device,
            device_id_type=MESH,
        ).start()

    @pl.when(is_root)
    def _():
        incoming = gathered.at[pl.ds(0, devices - 1)]
        pltpu.make_async_copy(incoming, incoming, stat_recv).wait()
        lane = lax.broadcasted_iota(jnp.int32, (1, 128), 1) & 15
        base = jnp.where(lane < 8, packed, 0.0)
        shifted = gathered[0:devices] - base
        sums = jnp.sum(shifted, axis=0, keepdims=True)
        between = jnp.sum(shifted * shifted, axis=0, keepdims=True)
        between = between - sums * sums * (1.0 / devices)
        variance = (sums + cells * pltpu.roll(between, 8, 1)) * (1.0 / (devices * cells))
        merged = jnp.where(
            lane < 8, base + sums * (1.0 / devices), lax.rsqrt(variance + EPSILON)
        )
        merged_row[...] = merged

    @pl.when(jnp.logical_not(is_root))
    def _():
        pltpu.make_async_copy(merged_row, merged_row, param_recv).wait()

    def targets(r):
        return [
            (z, 2 * chip + core)
            for z in range(rows)
            for chip in served[r]
            for core in (1, 0)
            if z > 0 or 2 * chip + core not in served
        ]

    for r in served:

        @pl.when(me == r)
        def _(r=r):
            for device in targets(r):
                send_params(device)

    merged = merged_row[...]
    quarter = lax.broadcasted_iota(jnp.int32, (1, 128), 1) >> 2 & 3
    spread = []
    for q in range(4):
        part = jnp.where(quarter == q, merged, 0.0)
        spread.append(part + sum(pltpu.roll(part, 4 * (j - q) % 128, 1) for j in range(4) if j != q))
    scalings = [affine[0, half : half + 1] * spread[2 + half] for half in range(2)]
    offsets = [affine[1, half : half + 1] - spread[half] * scalings[half] for half in range(2)]

    depth = 9 * 256
    newest = middle = oldest = 0.0
    for c in range(3):
        for half in range(2):
            for t in range(4):
                normed = windows[c, half, 8 + t * 112 : 120 + t * 112] * scalings[half] + offsets[half]
                halved = 0.5 * normed
                active = halved + halved * jnp.tanh(halved)
                even = active.astype(jnp.bfloat16)
                odd = active[8:104].astype(jnp.bfloat16)
                for b, cells in enumerate((even[0:96], odd, even[16:112])):
                    tap = (3 * b + c) * 256 + half * 128
                    patches[t * 96 : t * 96 + 96, tap : tap + 128] = cells
        for b in range(3):
            tap = (3 * b + c) * 256
            taps = slice(tap, tap + 256)
            newest += jnp.dot(
                patches[:, taps],
                weights[2 * depth + tap : 2 * depth + tap + 256],
                preferred_element_type=F32,
            )
            middle += jnp.dot(
                patches[0:288, taps],
                weights[depth + tap : depth + tap + 256],
                preferred_element_type=F32,
            )
            oldest += jnp.dot(
                patches[0:192, taps], weights[tap : tap + 256], preferred_element_type=F32
            )
    newest += jnp.concatenate([affine[2, 0:1], affine[2, 1:2]], axis=1)
    for t in range(4):
        m, o = max(t - 1, 0) * 96, max(t - 2, 0) * 96
        out_ref[t * 96 : t * 96 + 96] = (
            newest[t * 96 : t * 96 + 96] + middle[m : m + 96] + oldest[o : o + 96]
        ).astype(jnp.bfloat16)

    pltpu.make_async_copy(rim_out, rim_out, rim_send).wait()

    def wait_rows(count, semaphore):
        sent = gathered.at[pl.ds(0, count)]
        pltpu.make_async_copy(sent, sent, semaphore).wait()

    @pl.when(is_root)
    def _():
        wait_rows(len(served) - 1, stat_send)

    @pl.when(jnp.logical_not(is_root))
    def _():
        wait_rows(len(served), stat_send)

    for r in served:
        if targets(r):

            @pl.when(me == r)
            def _(r=r):
                wait_rows(len(targets(r)), param_send)


def solution(mesh):
    rows, cols = mesh.shape["row"], mesh.shape["col"]

    def body(latent, group_gain, group_shift, taps, kernel_bias):
        frames, height, breadth, channels = latent.shape
        cells = frames * height * breadth
        vmem = pl.BlockSpec(memory_space=pltpu.VMEM)
        remote = pl.BlockSpec(memory_space=pltpu.HBM)
        result = pl.pallas_call(
            functools.partial(kernel, rows, cols),
            out_shape=jax.ShapeDtypeStruct((cells, channels), jnp.bfloat16),
            in_specs=[remote] * 5,
            out_specs=vmem,
            scratch_shapes=[
                pltpu.VMEM((cells, channels), jnp.bfloat16),
                pltpu.VMEM((3, 2, 128), F32),
                pltpu.VMEM((27 * channels, channels), jnp.bfloat16),
                pltpu.VMEM((2, 768, 128), F32),
                pltpu.VMEM((192, channels), F32),
                pltpu.VMEM((192, channels), F32),
                pltpu.VMEM((1, 128), F32),
                pltpu.VMEM((rows * cols + 8, 128), F32),
                pltpu.VMEM((1, 128), F32),
                pltpu.VMEM((3, 2, 904, 128), F32),
                pltpu.VMEM((2, 2, 112, 128), F32),
                pltpu.VMEM((cells, 9 * channels), jnp.bfloat16),
                pltpu.SemaphoreType.DMA((3,)),
                pltpu.SemaphoreType.DMA,
                pltpu.SemaphoreType.DMA,
                pltpu.SemaphoreType.DMA,
                pltpu.SemaphoreType.DMA,
                pltpu.SemaphoreType.DMA,
                pltpu.SemaphoreType.DMA,
            ],
            compiler_params=pltpu.CompilerParams(
                collective_id=0, has_side_effects=True, vmem_limit_bytes=48 * 2**20
            ),
        )(
            pltpu.with_memory_space_constraint(latent.reshape(cells, channels), pltpu.HBM),
            pltpu.with_memory_space_constraint(group_gain.reshape(2, 128), pltpu.HBM),
            pltpu.with_memory_space_constraint(group_shift.reshape(2, 128), pltpu.HBM),
            pltpu.with_memory_space_constraint(taps.reshape(27 * channels, channels), pltpu.HBM),
            pltpu.with_memory_space_constraint(kernel_bias.reshape(2, 128), pltpu.HBM),
        )
        return result.reshape(frames, height, breadth, channels)

    return jax.shard_map(
        body,
        mesh=mesh,
        in_specs=(P(None, "row", "col", None), P(), P(), P(), P()),
        out_specs=P(None, "row", "col", None),
        check_vma=False,
    )
```

```python
import functools

import jax
import jax.numpy as jnp
from jax import lax
from jax.experimental import pallas as pl
from jax.experimental.pallas import tpu as pltpu
from jax.sharding import PartitionSpec as P

GROUP_CH = 16
EPSILON = 1e-06
MESH = pl.DeviceIdType.MESH
SIDES = (64, 112)
CORNERS = (160, 176, 192, 208)
F32 = jnp.float32


SERVED = {
    1: (0,),
    9: (4, 8, 5, 9),
    3: (1, 2, 6, 10),
    25: (12, 13, 14, 15),
    7: (3, 7, 11),
}


def roots_of(cols):
    if cols == 32:
        return SERVED
    return {1: (), 0: tuple(range(cols // 2))}


def group_total(values):
    lane = lax.broadcasted_iota(jnp.int32, values.shape, 1) & 15
    for stride in (1, 4):
        total = values
        for step in (stride, 2 * stride, 3 * stride):
            total = total + jnp.where(
                lane >= step, pltpu.roll(values, step, 1), pltpu.roll(values, 112 + step, 1)
            )
        values = total
    return values


def halves(values):
    return jnp.concatenate([values[:, :128], values[:, 128:]], axis=0)


def kernel(
    rows,
    cols,
    latent_hbm,
    gain_hbm,
    shift_hbm,
    weights_hbm,
    bias_hbm,
    out_ref,
    raw,
    affine,
    weights,
    own,
    rim_out,
    rim_in,
    stat_row,
    gathered,
    merged_row,
    windows,
    rims,
    patches,
    load_sem,
    rim_send,
    rim_recv,
    stat_send,
    stat_recv,
    param_send,
    param_recv,
):
    row, col = lax.axis_index("row"), lax.axis_index("col")
    devices = rows * cols
    me = row * cols + col
    served = roots_of(cols)
    is_root = functools.reduce(jnp.logical_or, [me == r for r in served])
    up, down = lax.rem(row + rows - 1, rows), lax.rem(row + 1, rows)
    left, right = lax.rem(col + cols - 1, cols), lax.rem(col + 1, cols)

    load = pltpu.make_async_copy(latent_hbm, raw, load_sem.at[0])
    load.start()

    barrier = pltpu.get_barrier_semaphore()
    for r in (up, row, down):
        for c in (left, col, right):
            if r is not row or c is not col:
                pl.semaphore_signal(barrier, inc=1, device_id=(r, c), device_id_type=MESH)

    @pl.when(is_root)
    def _():
        def greet(i, carry):
            far = lax.rem(rows // 2 + jnp.where(i & 1 == 0, i >> 1, rows - ((i + 1) >> 1)), rows)
            for c in range(cols):
                pl.semaphore_signal(barrier, inc=1, device_id=(far, c), device_id_type=MESH)
            return carry

        lax.fori_loop(0, rows - 1, greet, 0)
        for offset in range(1, cols):
            pl.semaphore_signal(
                barrier, inc=1, device_id=(0, (col + offset) & (cols - 1)), device_id_type=MESH
            )

    for i, source in enumerate((gain_hbm, shift_hbm, bias_hbm)):
        pltpu.make_async_copy(source, affine.at[i], load_sem.at[1]).start()
    load_weights = pltpu.make_async_copy(weights_hbm, weights, load_sem.at[2])
    load_weights.start()

    load.wait()
    values = raw[...].astype(F32)
    count = values.shape[0]
    own[0, 0:count] = values[:, :128]
    own[1, 0:count] = values[:, 128:]
    cells = float(count * GROUP_CH)
    first = values[0:1]
    shifted = values - first
    sums = halves(jnp.sum(shifted, axis=0, keepdims=True))
    squares = halves(jnp.sum(shifted * shifted, axis=0, keepdims=True))
    squares = squares - sums * sums * (1.0 / count)
    first = halves(first)
    place = lax.broadcasted_iota(jnp.int32, (2, 128), 1) & 15
    base = jnp.where(place == 0, first, 0.0)
    for stride in (1, 4):
        base = base + sum(pltpu.roll(base, j * stride, 1) for j in (1, 2, 3))
    sums = sums + count * (first - base)
    squares = squares + sums * sums * (1.0 / count)
    totals = group_total(jnp.concatenate([sums, squares], axis=0))
    means = base + totals[0:2] * (1.0 / cells)
    squares = totals[2:4] - totals[0:2] * totals[0:2] * (1.0 / cells)
    part = lax.broadcasted_iota(jnp.int32, (1, 128), 1) & 12
    packed = jnp.where(
        part < 8,
        jnp.where(part == 0, means[0:1], means[1:2]),
        jnp.where(part == 8, squares[0:1], squares[1:2]),
    )
    stat_row[...] = packed

    for end in (0, 88):
        edge = [values[t * 96 + end : t * 96 + end + 8] for t in range(4)]
        at = 32 * (end > 0)
        rim_out[at : at + 32] = jnp.concatenate(edge, axis=0).astype(jnp.bfloat16)
    for side, cell in ((0, 0), (1, 7)):
        for half in range(2):
            lanes = slice(half * 128, half * 128 + 128)
            at = SIDES[side]
            rim_out[at : at + 48, lanes] = own[half, pl.ds(cell, 48, stride=8), :].astype(jnp.bfloat16)
            for end, place in ((0, 0), (1, 88)):
                at = CORNERS[2 * end + side]
                corner = own[half, pl.ds(place + cell, 4, stride=96), :]
                rim_out[at : at + 16, lanes] = jnp.concatenate(
                    [corner, jnp.zeros((12, 128), F32)], axis=0
                ).astype(jnp.bfloat16)

    def send_stats(c):
        pltpu.make_async_remote_copy(
            src_ref=stat_row,
            dst_ref=gathered.at[pl.ds(me, 1)],
            send_sem=stat_send,
            recv_sem=stat_recv,
            device_id=(0, c),
            device_id_type=MESH,
        ).start()

    @pl.when(is_root)
    def _():
        pl.semaphore_wait(barrier, 7 + len(served))
        gathered[pl.ds(me, 1)] = packed
        for r in served:
            pl.when(me != r)(functools.partial(send_stats, r))

    @pl.when(jnp.logical_not(is_root))
    def _():
        pl.semaphore_wait(barrier, 8 + len(served))
        for r in served:
            send_stats(r)

    for source, target, size, device in (
        (0, 32, 32, (up, col)),
        (32, 0, 32, (down, col)),
        (SIDES[0], SIDES[1], 48, (row, left)),
        (SIDES[1], SIDES[0], 48, (row, right)),
        (CORNERS[0], CORNERS[3], 16, (up, left)),
        (CORNERS[1], CORNERS[2], 16, (up, right)),
        (CORNERS[2], CORNERS[1], 16, (down, left)),
        (CORNERS[3], CORNERS[0], 16, (down, right)),
    ):
        pltpu.make_async_remote_copy(
            src_ref=rim_out.at[pl.ds(source, size)],
            dst_ref=rim_in.at[pl.ds(target, size)],
            send_sem=rim_send,
            recv_sem=rim_recv,
            device_id=device,
            device_id_type=MESH,
        ).start()

    pltpu.make_async_copy(rim_in, rim_in, rim_recv).wait()

    at_row = (row == 0, row == rows - 1)
    at_col = (col == 0, col == cols - 1)
    for half in range(2):
        lanes = slice(half * 128, half * 128 + 128)
        for t in range(4):
            base = 8 + t * 112
            windows[1, half, base + 8 : base + 104] = own[half, t * 96 : t * 96 + 96]
            for side, at, edge in ((0, base, 0), (1, base + 104, 88)):
                windows[1, half, at : at + 8] = jnp.where(
                    at_row[side],
                    own[half, t * 96 + edge : t * 96 + edge + 8],
                    rim_in[side * 32 : side * 32 + 32, lanes].astype(F32)[t * 8 : t * 8 + 8],
                )
        for side, cell in ((0, 0), (1, 7)):
            column = jnp.where(
                at_col[side],
                own[half, pl.ds(cell, 48, stride=8), :],
                rim_in[SIDES[side] : SIDES[side] + 48, lanes].astype(F32),
            )
            for t in range(4):
                rims[side, half, t * 14 + 1 : t * 14 + 13] = column[t * 12 : t * 12 + 12]
            for end, place, inner in ((0, 0, 1), (1, 13, 12)):
                corner = CORNERS[2 * end + side]
                rims[side, half, pl.ds(place, 4, stride=14), :] = jnp.where(
                    at_row[end],
                    rims[side, half, pl.ds(inner, 4, stride=14), :],
                    jnp.where(
                        at_col[side],
                        windows[1, half, pl.ds(8 + place * 8 + cell, 4, stride=112), :],
                        rim_in[corner : corner + 16, lanes].astype(F32)[0:4],
                    ),
                )
        for t in range(4):
            base = 8 + t * 112
            windows[0, half, base : base + 112] = windows[1, half, base - 1 : base + 111]
            windows[2, half, base : base + 112] = windows[1, half, base + 1 : base + 113]
        windows[0, half, pl.ds(8, 56, stride=8), :] = rims[0, half, 0:56]
        windows[2, half, pl.ds(15, 56, stride=8), :] = rims[1, half, 0:56]

    pltpu.make_async_copy(affine, affine, load_sem.at[1]).wait()
    load_weights.wait()

    def send_params(device):
        pltpu.make_async_remote_copy(
            src_ref=merged_row,
            dst_ref=merged_row,
            send_sem=param_send,
            recv_sem=param_recv,
            device_id=device,
            device_id_type=MESH,
        ).start()

    @pl.when(is_root)
    def _():
        incoming = gathered.at[pl.ds(0, devices - 1)]
        pltpu.make_async_copy(incoming, incoming, stat_recv).wait()
        lane = lax.broadcasted_iota(jnp.int32, (1, 128), 1) & 15
        base = jnp.where(lane < 8, packed, 0.0)
        shifted = gathered[0:devices] - base
        sums = jnp.sum(shifted, axis=0, keepdims=True)
        between = jnp.sum(shifted * shifted, axis=0, keepdims=True)
        between = between - sums * sums * (1.0 / devices)
        variance = (sums + cells * pltpu.roll(between, 8, 1)) * (1.0 / (devices * cells))
        merged = jnp.where(
            lane < 8, base + sums * (1.0 / devices), lax.rsqrt(variance + EPSILON)
        )
        merged_row[...] = merged

    @pl.when(jnp.logical_not(is_root))
    def _():
        pltpu.make_async_copy(merged_row, merged_row, param_recv).wait()

    def targets(r):
        return [
            (z, 2 * chip + core)
            for z in range(rows)
            for chip in served[r]
            for core in (1, 0)
            if z > 0 or 2 * chip + core not in served
        ]

    for r in served:

        @pl.when(me == r)
        def _(r=r):
            for device in targets(r):
                send_params(device)

    merged = merged_row[...]
    quarter = lax.broadcasted_iota(jnp.int32, (1, 128), 1) >> 2 & 3
    spread = []
    for q in range(4):
        part = jnp.where(quarter == q, merged, 0.0)
        spread.append(part + sum(pltpu.roll(part, 4 * (j - q) % 128, 1) for j in range(4) if j != q))
    scalings = [affine[0, half : half + 1] * spread[2 + half] for half in range(2)]
    offsets = [affine[1, half : half + 1] - spread[half] * scalings[half] for half in range(2)]

    depth = 9 * 256
    newest = middle = oldest = 0.0
    for c in range(3):
        for half in range(2):
            for t in range(4):
                normed = windows[c, half, 8 + t * 112 : 120 + t * 112] * scalings[half] + offsets[half]
                halved = 0.5 * normed
                active = halved + halved * jnp.tanh(halved)
                even = active.astype(jnp.bfloat16)
                odd = active[8:104].astype(jnp.bfloat16)
                for b, cells in enumerate((even[0:96], odd, even[16:112])):
                    tap = (3 * b + c) * 256 + half * 128
                    patches[t * 96 : t * 96 + 96, tap : tap + 128] = cells
        for b in range(3):
            tap = (3 * b + c) * 256
            taps = slice(tap, tap + 256)
            newest += jnp.dot(
                patches[:, taps],
                weights[2 * depth + tap : 2 * depth + tap + 256],
                preferred_element_type=F32,
            )
            middle += jnp.dot(
                patches[0:288, taps],
                weights[depth + tap : depth + tap + 256],
                preferred_element_type=F32,
            )
            oldest += jnp.dot(
                patches[0:192, taps], weights[tap : tap + 256], preferred_element_type=F32
            )
    newest += jnp.concatenate([affine[2, 0:1], affine[2, 1:2]], axis=1)
    for t in range(4):
        m, o = max(t - 1, 0) * 96, max(t - 2, 0) * 96
        out_ref[t * 96 : t * 96 + 96] = (
            newest[t * 96 : t * 96 + 96] + middle[m : m + 96] + oldest[o : o + 96]
        ).astype(jnp.bfloat16)

    pltpu.make_async_copy(rim_out, rim_out, rim_send).wait()

    def wait_rows(count, semaphore):
        sent = gathered.at[pl.ds(0, count)]
        pltpu.make_async_copy(sent, sent, semaphore).wait()

    @pl.when(is_root)
    def _():
        wait_rows(len(served) - 1, stat_send)

    @pl.when(jnp.logical_not(is_root))
    def _():
        wait_rows(len(served), stat_send)

    for r in served:
        if targets(r):

            @pl.when(me == r)
            def _(r=r):
                wait_rows(len(targets(r)), param_send)


def solution(mesh):
    rows, cols = mesh.shape["row"], mesh.shape["col"]

    def body(latent, group_gain, group_shift, taps, kernel_bias):
        frames, height, breadth, channels = latent.shape
        cells = frames * height * breadth
        vmem = pl.BlockSpec(memory_space=pltpu.VMEM)
        remote = pl.BlockSpec(memory_space=pltpu.HBM)
        result = pl.pallas_call(
            functools.partial(kernel, rows, cols),
            out_shape=jax.ShapeDtypeStruct((cells, channels), jnp.bfloat16),
            in_specs=[remote] * 5,
            out_specs=vmem,
            scratch_shapes=[
                pltpu.VMEM((cells, channels), jnp.bfloat16),
                pltpu.VMEM((3, 2, 128), F32),
                pltpu.VMEM((27 * channels, channels), jnp.bfloat16),
                pltpu.VMEM((2, 768, 128), F32),
                pltpu.VMEM((224, channels), jnp.bfloat16),
                pltpu.VMEM((224, channels), jnp.bfloat16),
                pltpu.VMEM((1, 128), F32),
                pltpu.VMEM((rows * cols + 8, 128), F32),
                pltpu.VMEM((1, 128), F32),
                pltpu.VMEM((3, 2, 904, 128), F32),
                pltpu.VMEM((2, 2, 112, 128), F32),
                pltpu.VMEM((cells, 9 * channels), jnp.bfloat16),
                pltpu.SemaphoreType.DMA((3,)),
                pltpu.SemaphoreType.DMA,
                pltpu.SemaphoreType.DMA,
                pltpu.SemaphoreType.DMA,
                pltpu.SemaphoreType.DMA,
                pltpu.SemaphoreType.DMA,
                pltpu.SemaphoreType.DMA,
            ],
            compiler_params=pltpu.CompilerParams(
                collective_id=0, has_side_effects=True, vmem_limit_bytes=48 * 2**20
            ),
        )(
            pltpu.with_memory_space_constraint(latent.reshape(cells, channels), pltpu.HBM),
            pltpu.with_memory_space_constraint(group_gain.reshape(2, 128), pltpu.HBM),
            pltpu.with_memory_space_constraint(group_shift.reshape(2, 128), pltpu.HBM),
            pltpu.with_memory_space_constraint(taps.reshape(27 * channels, channels), pltpu.HBM),
            pltpu.with_memory_space_constraint(kernel_bias.reshape(2, 128), pltpu.HBM),
        )
        return result.reshape(frames, height, breadth, channels)

    return jax.shard_map(
        body,
        mesh=mesh,
        in_specs=(P(None, "row", "col", None), P(), P(), P(), P()),
        out_specs=P(None, "row", "col", None),
        check_vma=False,
    )
```
